32 devices in a mesh: batch: 8 (over z, x), blk: 4 (over y, core).
Axes of the slice: x: 2, y: 2, z: 4, core: 2. Of those that a mesh axis runs over, the one named last changes fastest.
Arguments:
- hidden_in: bfloat16 [16, 512, 512], P('batch', 'blk'), may hold values from -6 to 6
- cotangent: bfloat16 [16, 512, 512], P('batch', 'blk'), may hold values from -6 to 6
- lengths: int32 [16, 4], P('batch'), may hold values from 1 to 448, 512 in all within a row
- norm_gain: float32 [2, 2, 512], replicated, may hold values from 0.1 to 1.9
- conv_weight: float32 [2, 4, 512], replicated, may hold values from -3 to 3
- gate_bias: float32 [2, 1024], replicated, may hold values from -9 to -2
- in_weight: bfloat16 [2, 512, 2048], replicated, may hold values from -0.25 to 0.25
- out_weight: bfloat16 [2, 1024, 512], replicated, may hold values from -0.375 to 0.375
- up_weight: bfloat16 [2, 512, 2048], replicated, may hold values from -0.25 to 0.25
- down_weight: bfloat16 [2, 2048, 512], replicated, may hold values from -0.125 to 0.125
Outputs:
- mixed: bfloat16 [16, 512, 512], P('batch', 'blk')
- input_grad: bfloat16 [16, 512, 512], P('batch', 'blk')
- grad_gain: float32 [2, 2, 512], replicated
- grad_conv: float32 [2, 4, 512], replicated
- grad_bias: float32 [2, 1024], replicated
- grad_in_proj: float32 [2, 512, 2048], replicated
- grad_out_proj: float32 [2, 1024, 512], replicated
- grad_up: float32 [2, 512, 2048], replicated
- grad_down: float32 [2, 2048, 512], replicated
The draws below stay inside these ranges and needn't reach their ends.
Inputs may be any that keep to these rules, and one draw needn't show every extreme that they name: In each row the 4 lengths sum to 512, and one of them is exactly 448.
All inputs are finite; a program needn't handle non-finite values.
Results may differ from the reference program's by a relative error of at most 0.023.
Values may be sent and summed in bfloat16 or wider, within the bound.
No kernel may reach another device: no remote copies, remote signals or barrier semaphores. Data moves between devices by JAX's collectives and lax.ppermute only.
A program may use at most 320 MiB of HBM per device.

```python
import math
import jax
import jax.numpy as jnp
import numpy as np
from jax import lax

D = 512
H = 1024
FF = 2048
KW = 4
DOCS = 4
LAYERS = 2
SPAN = 128
ROWS = 16
LEN = 512


def draw_gate_bias(key, part):
    key = jax.random.fold_in(key, 11)
    return jax.random.uniform(key, (LAYERS, H), jnp.float32, -9.0, -2.0)


def shard_levels(key, shape, cuts, low, high):
    factor_of = 1.0
    for axis_at, parts in cuts:
        heights = jax.random.uniform(jax.random.fold_in(jax.random.fold_in(key, 6), axis_at), (parts,), jnp.float32, low / len(cuts), high / len(cuts))
        factor_of = factor_of * jnp.repeat(jnp.exp(heights), shape[axis_at] // parts).reshape((-1,) + (1,) * (len(shape) - 1 - axis_at))
    return factor_of


def profile(amount, total, bound, slope):
    loads = [(1 << 20) // math.isqrt(standing ** slope) + 1 for standing in range(2, amount + 1)]
    spare, holding = total - bound - (amount - 1), [1] * (amount - 1)
    while spare > 0:
        free = [i for i in range(amount - 1) if holding[i] < bound]
        pool, budget = sum([loads[i] for i in free]), spare
        for i in free:
            addition = min(bound - holding[i], max(1, budget * loads[i] // pool), spare)
            holding[i] = holding[i] + addition
            spare = spare - addition
    return np.array([bound] + holding)


def uneven(rng, number_of, total, reach, slope):
    if number_of == 2:
        one = jax.random.randint(rng, (), max(1, total - reach), min(reach, total - 1) + 1)
        return jnp.stack([one, total - one])
    sizes = jnp.asarray(profile(number_of, total, reach, slope), jnp.int32)
    couples = (number_of - 1) // 2
    donor, receiver = sizes[1:1 + 2 * couples:2], sizes[2:2 + 2 * couples:2]
    room = jnp.minimum(donor - 1, reach - receiver)
    shifted = jax.random.randint(jax.random.fold_in(rng, 1), (couples,), 0, 1 << 20) % (room + 1)
    sizes = sizes.at[1:1 + 2 * couples:2].set(donor - shifted).at[2:2 + 2 * couples:2].set(receiver + shifted)
    return sizes[jax.random.permutation(jax.random.fold_in(rng, 2), number_of)]


def gaussian(rng, shape, scale, bound, cuts=(), kind=jnp.bfloat16):
    factor_of = shard_levels(rng, shape, cuts, -0.22, 0.18) if cuts else 1.0
    values = jax.random.normal(rng, shape, jnp.float32) * scale * factor_of
    return jnp.minimum(jnp.maximum(values, -bound), bound).astype(kind)


def setup_inputs(seed: int = 0) -> dict:
    keys = jax.random.split(jax.random.key(seed), 11)
    return {
        "hidden_in": gaussian(keys[0], (ROWS, LEN, D), 1.0, 6.0, ((0, 8), (1, 4))),
        "cotangent": gaussian(keys[1], (ROWS, LEN, D), 1.0, 6.0, ((0, 8), (1, 4))),
        "lengths": jax.vmap(lambda own: uneven(own, DOCS, LEN, LEN - SPAN // 2, 2))(jax.random.split(keys[2], ROWS)).reshape((ROWS, DOCS)).astype(jnp.int32),
        "norm_gain": jnp.clip(1.0 + 0.18 * jax.random.normal(keys[3], (LAYERS, 2, D), jnp.float32), 0.1, 1.9),
        "conv_weight": gaussian(keys[4], (LAYERS, KW, D), 0.5, 3.0, (), jnp.float32),
        "gate_bias": draw_gate_bias(jax.random.fold_in(keys[10], 71), 0),
        "in_weight": gaussian(keys[6], (LAYERS, D, 2 * H), D ** -0.5, 0.25),
        "out_weight": gaussian(keys[7], (LAYERS, H, D), (H // 4) ** -0.5, 0.375),
        "up_weight": gaussian(keys[8], (LAYERS, D, FF), D ** -0.5, 0.25),
        "down_weight": gaussian(keys[9], (LAYERS, FF, D), FF ** -0.5, 0.125),
    }


@jax.custom_vjp
def low(v):
    return lax.optimization_barrier(v.astype(jnp.bfloat16)).astype(jnp.float32)

@jax.custom_vjp
def low_back(v):
    return v

def low_keep(v):
    return (low(v), None)

def low_pass(kept, grad):
    return (grad,)

def back_keep(v):
    return (v, None)

def back_low(kept, grad):
    return (low(grad),)
low.defvjp(low_keep, low_pass)
low_back.defvjp(back_keep, back_low)

def normalize(values, gains):
    return values * lax.rsqrt(lax.optimization_barrier(jnp.mean(values * values, axis=-1, keepdims=True)) + 1e-06) * gains

def candidate_fn(values):
    return jnp.where(values >= 0, values + 0.5, jax.nn.sigmoid(values))

def doc_offsets(lengths, start_pos, extent):
    starts = jnp.cumsum(lengths, axis=1, dtype=jnp.int32) - lengths
    places = start_pos + jnp.arange(extent, dtype=jnp.int32)
    before = starts[:, None, :] <= places[None, :, None]
    latest = lax.optimization_barrier(jnp.max(jnp.where(before, starts[:, None, :], 0), axis=2))
    return places[None, :] - latest

def convolve(extended, conv_taps, offsets):
    extent = offsets.shape[1]
    tap_count = conv_taps.shape[0]
    result = jnp.zeros((extended.shape[0], extent, extended.shape[2]), jnp.float32)
    for tap_index in range(tap_count):
        begin = tap_count - 1 - tap_index
        window = extended[:, begin:begin + extent].astype(jnp.float32)
        valid = (offsets >= tap_index)[:, :, None].astype(jnp.float32)
        result = result + conv_taps[tap_index] * window * valid
    return result

def merge_affine_pairs(earlier, subsequent):
    return (earlier[0] * subsequent[0], subsequent[0] * earlier[1] + subsequent[1])

def matmul(left, right):
    return jnp.einsum('rtd,de->rte', left, right, precision=lax.Precision.HIGHEST)

def layer(hidden, offsets, gains, conv_taps, biases, w_in, w_out, w_up, w_down):
    tap_count = conv_taps.shape[0]
    hidden_units = w_out.shape[0]
    normed = low(normalize(hidden, gains[0]))
    extended = jnp.pad(normed, ((0, 0), (tap_count - 1, 0), (0, 0)))
    conv_out = low(convolve(extended, conv_taps, offsets))
    projected = low_back(matmul(conv_out, w_in))
    update = jax.nn.sigmoid(projected[..., :hidden_units] + biases)
    candidate = candidate_fn(projected[..., hidden_units:])
    retain = (1.0 - update) * (offsets > 0)[:, :, None].astype(jnp.float32)
    state = lax.associative_scan(merge_affine_pairs, (retain, update * candidate), axis=1)[1]
    middle = hidden + low_back(matmul(low(state), w_out))
    second = low(normalize(middle, gains[1]))
    before_act = low_back(matmul(second, w_up))
    activated = low(jax.nn.gelu(before_act, approximate=False))
    return middle + low_back(matmul(activated, w_down))

def forward(hidden, offsets, params):
    for layer_index in range(LAYERS):
        hidden = layer(hidden, offsets, *[member[layer_index] for member in params])
    return hidden

def reference(hidden_in, cotangent, lengths, norm_gain, conv_weight, gate_bias, in_weight, out_weight, up_weight, down_weight):
    row_count = hidden_in.shape[0]
    extent = hidden_in.shape[1]
    group = math.gcd(row_count, max(1, 4096 // extent))
    groups = row_count // group
    params = tuple((member.astype(jnp.float32) for member in (norm_gain, conv_weight, gate_bias, in_weight, out_weight, up_weight, down_weight)))

    def one_group(totals, inputs):
        hidden, cot_rows, row_lengths = inputs
        offsets = doc_offsets(row_lengths, 0, extent)
        result, pullback = jax.vjp(lambda values, weights: forward(values, offsets, weights), hidden.astype(jnp.float32), params)
        grad_hidden, grad_params = pullback(cot_rows.astype(jnp.float32))
        totals = jax.tree.map(jnp.add, totals, grad_params)
        return (totals, (result.astype(jnp.bfloat16), grad_hidden.astype(jnp.bfloat16)))
    inputs = (hidden_in.reshape(groups, group, extent, -1), cotangent.reshape(groups, group, extent, -1), lengths.reshape(groups, group, -1))
    zeros = jax.tree.map(jnp.zeros_like, params)
    totals, (results, grads) = lax.scan(one_group, zeros, inputs)
    return (results.reshape(hidden_in.shape), grads.reshape(hidden_in.shape), totals[0], totals[1], totals[2], totals[3], totals[4], totals[5], totals[6])
```

```python
import functools

import jax
import jax.numpy as jnp
from jax import lax
from jax.experimental import pallas as pl
from jax.experimental.pallas import tpu as pltpu
from jax.sharding import PartitionSpec as P

AXES = ("batch", "blk")
EPS = 1e-6
CHUNK = 256
F32 = jnp.float32
BF16 = jnp.bfloat16
VMEM = 40 * 1024 * 1024


def spec():
    return pl.BlockSpec(memory_space=pltpu.VMEM)


def smem():
    return pl.BlockSpec(memory_space=pltpu.SMEM)


def call(body, outs, args, scalars=1, scratch=(), name=None):
    return pl.pallas_call(
        body,
        out_shape=tuple(jax.ShapeDtypeStruct(s, d) for s, d in outs),
        in_specs=[smem()] * scalars + [spec()] * (len(args) - scalars),
        out_specs=tuple(spec() for _ in outs),
        scratch_shapes=scratch,
        compiler_params=pltpu.CompilerParams(vmem_limit_bytes=VMEM),
        name=name,
    )(*args)


def dot(a, b, ca=1, cb=0):
    return lax.dot_general(a, b, (((ca,), (cb,)), ((), ())), preferred_element_type=F32)


def offsets_of(info, row, span):
    docs = DOCS
    pos = info[0] + lax.broadcasted_iota(jnp.int32, (span, 1), 0)
    latest = jnp.zeros((span, 1), jnp.int32)
    for j in range(docs):
        start = info[2 + row * docs + j]
        latest = jnp.maximum(latest, jnp.where(start <= pos, start, 0))
    return pos - latest


DOCS = 4


def rms(values):
    return lax.rsqrt(jnp.mean(values * values, axis=-1, keepdims=True) + EPS)


def low(values):
    return values.astype(BF16).astype(F32)


def scan_forward(a, b, put):
    span, cols = a.shape
    a3, b3 = a.reshape(span // 8, 8, cols), b.reshape(span // 8, 8, cols)
    place = lax.broadcasted_iota(jnp.int32, (1, 8, cols), 1)
    for s in (1, 2, 4):
        inside = place >= s
        a_prev = jnp.where(inside, pltpu.roll(a3, s, 1), 1.0)
        b_prev = jnp.where(inside, pltpu.roll(b3, s, 1), 0.0)
        b3 = b3 + a3 * b_prev
        a3 = a3 * a_prev
    through = jnp.ones((1, cols), F32)
    state = jnp.zeros((1, cols), F32)
    for g in range(span // 8):
        st = b3[g] + a3[g] * state
        th = a3[g] * through
        put(8 * g, th, st)
        through, state = th[7:8], st[7:8]
    return through, state


def scan_backward(a, g, put):
    span, cols = a.shape
    b = a * g
    a3, b3 = a.reshape(span // 8, 8, cols), b.reshape(span // 8, 8, cols)
    place = lax.broadcasted_iota(jnp.int32, (1, 8, cols), 1)
    for s in (1, 2, 4):
        inside = place < 8 - s
        a_next = jnp.where(inside, pltpu.roll(a3, 8 - s, 1), 1.0)
        b_next = jnp.where(inside, pltpu.roll(b3, 8 - s, 1), 0.0)
        b3 = b3 + a3 * b_next
        a3 = a3 * a_next
    last = lax.broadcasted_iota(jnp.int32, (8, cols), 0) == 7
    reach = jnp.ones((1, cols), F32)
    value = jnp.zeros((1, cols), F32)
    for i in reversed(range(span // 8)):
        va = b3[i] + a3[i] * value
        re = a3[i] * reach
        put(8 * i, jnp.where(last, reach, pltpu.roll(re, 7, 0)), jnp.where(last, value, pltpu.roll(va, 7, 0)))
        reach, value = re[0:1], va[0:1]
    return reach, value


def gates_body(info, x, xh, gain, taps, bias, w_in, u_o, cand_o, c2_o, th_o, pa_o, conv_o, sum_o, ext):
    rows, span, _ = x.shape
    hidden = u_o.shape[1]
    kw = taps.shape[0]
    g0 = gain[0:1, :]
    for r in range(rows):
        off = offsets_of(info, r, span)
        xm = x[r].astype(F32)
        ext[8 : 8 + span, :] = low(xm * rms(xm) * g0)
        xv = xh[r].astype(F32)
        ext[0:8, :] = low(xv * rms(xv) * g0)
        acc = taps[0:1, :] * ext[8 : 8 + span, :]
        for k in range(1, kw):
            acc = acc + taps[k : k + 1, :] * ext[8 - k : 8 - k + span, :] * (off >= k).astype(F32)
        conv_o[r * span : (r + 1) * span, :] = acc.astype(BF16)
    conv = conv_o[...]
    sum_o[...] = jnp.zeros(sum_o.shape, F32)
    for c in range(hidden // CHUNK):
        lo, hi = c * CHUNK, (c + 1) * CHUNK
        pu = dot(conv, w_in[:, lo:hi]) + bias[0:1, lo:hi]
        pc = dot(conv, w_in[:, hidden + lo : hidden + hi])
        u = jax.nn.sigmoid(pu)
        sg = jax.nn.sigmoid(pc)
        up = pc >= 0
        cand = jnp.where(up, pc + 0.5, sg)
        u_o[:, lo:hi] = u
        cand_o[:, lo:hi] = cand
        c2_o[:, lo:hi] = u * jnp.where(up, 1.0, sg * (1.0 - sg))
        b = u * cand
        for r in range(rows):
            alive = (offsets_of(info, r, span) > 0).astype(F32)
            base = r * span

            def put(row, th, st, base=base, lo=lo, hi=hi):
                th_o[base + row : base + row + 8, lo:hi] = th
                pa_o[base + row : base + row + 8, lo:hi] = st

            th, st = scan_forward((1.0 - u[base : base + span]) * alive, b[base : base + span], put)
            sum_o[2 * r : 2 * r + 1, lo:hi] = th
            sum_o[2 * r + 1 : 2 * r + 2, lo:hi] = st


def gates(info, x, xh, gain, taps, bias, w_in):
    rows, span, d = x.shape
    h = bias.shape[1]
    t = rows * span
    return call(
        gates_body,
        [((t, h), F32)] * 5 + [((t, d), BF16), ((8, h), F32)],
        (info, x, xh, gain, taps, bias, w_in),
        scratch=[pltpu.VMEM((span + 8, d), F32)],
        name="gates",
    )


def mix_body(
    blocks, span, info, x, sums, th, pa, u, cand, gain, w_out, w_up, w_down,
    state_o, c1_o, mid_o, sec_o, act_o, gp_o, out_o,
):
    rows = th.shape[0] // span
    hidden, d = w_out.shape
    ff = w_up.shape[1]
    me = info[1]
    mid = []
    for r in range(rows):
        base = r * span
        alive = (offsets_of(info, r, span) > 0).astype(F32)
        first = lax.broadcasted_iota(jnp.int32, (span, CHUNK), 0) == 0
        for c in range(hidden // CHUNK):
            lo, hi = c * CHUNK, (c + 1) * CHUNK
            enter = jnp.zeros((1, CHUNK), F32)
            for i in range(blocks - 1):
                stepped = sums[i, 2 * r : 2 * r + 1, lo:hi] * enter + sums[i, 2 * r + 1 : 2 * r + 2, lo:hi]
                enter = jnp.where(i < me, stepped, enter)
            st = pa[base : base + span, lo:hi] + th[base : base + span, lo:hi] * enter
            prev = jnp.where(first, enter, pltpu.roll(st, 1, 0))
            uu = u[base : base + span, lo:hi]
            c1_o[base : base + span, lo:hi] = (cand[base : base + span, lo:hi] - alive * prev) * uu * (1.0 - uu)
            state_o[base : base + span, lo:hi] = st.astype(BF16)
        mid.append(x[r].astype(F32))
    m = jnp.concatenate(mid, axis=0) + dot(state_o[...], w_out[...])
    mid_o[...] = m
    sec = (m * rms(m) * gain[1:2, :]).astype(BF16)
    sec_o[...] = sec
    step = 512
    out = m
    for c in range(ff // step):
        lo, hi = c * step, (c + 1) * step
        v = dot(sec, w_up[:, lo:hi])
        half = 0.5 * (1.0 + lax.erf(v * 0.7071067811865476))
        act = (v * half).astype(BF16)
        act_o[:, lo:hi] = act
        gp_o[:, lo:hi] = half + v * (0.3989422804014327 * jnp.exp(-0.5 * v * v))
        out = out + dot(act, w_down[lo:hi, :])
    out_o[...] = out


def mix(info, blocks, x, sums, th, pa, u, cand, gain, w_out, w_up, w_down):
    rows, span, d = x.shape
    t, h = th.shape
    ff = w_up.shape[1]
    return call(
        functools.partial(mix_body, blocks, span),
        [((t, h), BF16), ((t, h), F32), ((t, d), F32), ((t, d), BF16), ((t, ff), BF16), ((t, ff), F32), ((t, d), F32)],
        (info, x, sums, th, pa, u, cand, gain, w_out, w_up, w_down),
        name="mix",
    )


def mlp_back_body(
    span, info, g, gp, mid, u, gain, w_out, w_up, w_down,
    low_o, pre_o, gmid_o, branch_o, reach_o, adj_o, sum_o, gain_o,
):
    rows = g.shape[0] // span
    hidden, d = w_out.shape
    ff = w_up.shape[1]
    gf = g[...].astype(F32)
    gl = gf.astype(BF16)
    low_o[...] = gl
    step = 512
    gs = jnp.zeros(gf.shape, F32)
    for c in range(ff // step):
        lo, hi = c * step, (c + 1) * step
        pre = (dot(gl, w_down[lo:hi, :], 1, 1) * gp[:, lo:hi]).astype(BF16)
        pre_o[:, lo:hi] = pre
        gs = gs + dot(pre, w_up[:, lo:hi], 1, 1)
    m = mid[...]
    rr = rms(m)
    xhat = m * rr
    gain_o[...] = jnp.broadcast_to(jnp.sum(gs * xhat, axis=0, keepdims=True), gain_o.shape)
    e = gs * gain[1:2, :]
    gm = gf + rr * (e - xhat * jnp.mean(e * xhat, axis=-1, keepdims=True))
    gmid_o[...] = gm
    branch_o[...] = gm.astype(BF16)
    branch = branch_o[...]
    sum_o[...] = jnp.zeros(sum_o.shape, F32)
    for c in range(hidden // CHUNK):
        lo, hi = c * CHUNK, (c + 1) * CHUNK
        gstate = dot(branch, w_out[lo:hi, :], 1, 1)
        for r in range(rows):
            base = r * span
            alive = (offsets_of(info, r, span) > 0).astype(F32)
            gst = gstate[base : base + span]

            def put(row, re, va, base=base, lo=lo, hi=hi, gst=gst):
                reach_o[base + row : base + row + 8, lo:hi] = re
                adj_o[base + row : base + row + 8, lo:hi] = gst[row : row + 8] + va

            re, va = scan_backward((1.0 - u[base : base + span, lo:hi]) * alive, gst, put)
            sum_o[2 * r : 2 * r + 1, lo:hi] = re
            sum_o[2 * r + 1 : 2 * r + 2, lo:hi] = va


def mlp_back(info, span, g, gp, mid, u, gain, w_out, w_up, w_down):
    t, d = mid.shape
    h, ff = u.shape[1], gp.shape[1]
    return call(
        functools.partial(mlp_back_body, span),
        [
            ((t, d), BF16), ((t, ff), BF16), ((t, d), F32), ((t, d), BF16), ((t, h), F32), ((t, h), F32), ((8, h), F32), ((8, d), F32),
        ],
        (info, g, gp, mid, u, gain, w_out, w_up, w_down),
        name="mlp_back",
    )


def gates_back_body(
    blocks, info, x, xh, sums, reach, adj, c1, c2, gain, taps, w_in,
    proj_o, gn_o, ret_o, bias_o, taps_o, ext, gext,
):
    rows, span, d = x.shape
    hidden = c1.shape[1]
    kw = taps.shape[0]
    me = info[1]
    t = rows * span
    for c in range(hidden // CHUNK):
        lo, hi = c * CHUNK, (c + 1) * CHUNK
        total = jnp.zeros((1, CHUNK), F32)
        for r in range(rows):
            base = r * span
            enter = jnp.zeros((1, CHUNK), F32)
            for i in reversed(range(1, blocks)):
                stepped = sums[i, 2 * r : 2 * r + 1, lo:hi] * enter + sums[i, 2 * r + 1 : 2 * r + 2, lo:hi]
                enter = jnp.where(i > me, stepped, enter)
            ad = adj[base : base + span, lo:hi] + reach[base : base + span, lo:hi] * enter
            gl = ad * c1[base : base + span, lo:hi]
            total = total + jnp.sum(gl, axis=0, keepdims=True)
            proj_o[base : base + span, lo:hi] = gl.astype(BF16)
            proj_o[base : base + span, hidden + lo : hidden + hi] = (ad * c2[base : base + span, lo:hi]).astype(BF16)
        bias_o[:, lo:hi] = jnp.broadcast_to(total, (8, CHUNK))
    gci = dot(proj_o[...], w_in[...], 1, 1)
    g0 = gain[0:1, :]
    taps_o[...] = jnp.zeros(taps_o.shape, F32)
    for r in range(rows):
        base = r * span
        off = offsets_of(info, r, span)
        xm = x[r].astype(F32)
        ext[8 : 8 + span, :] = low(xm * rms(xm) * g0)
        xv = xh[r].astype(F32)
        ext[0:8, :] = low(xv * rms(xv) * g0)
        gr = gci[base : base + span]
        gext[...] = jnp.zeros(gext.shape, F32)
        gext[8 : 8 + span, :] = gr * taps[0:1, :]
        taps_o[0:1, :] = taps_o[0:1, :] + jnp.sum(gr * ext[8 : 8 + span, :], axis=0, keepdims=True)
        for k in range(1, kw):
            gk = gr * (off >= k).astype(F32)
            taps_o[k : k + 1, :] = taps_o[k : k + 1, :] + jnp.sum(gk * ext[8 - k : 8 - k + span, :], axis=0, keepdims=True)
            gext[8 - k : 8 - k + span, :] = gext[8 - k : 8 - k + span, :] + gk * taps[k : k + 1, :]
        gn_o[base : base + span, :] = gext[8 : 8 + span, :]
        ret_o[8 * r : 8 * r + 8, :] = gext[0:8, :]


def gates_back(info, blocks, x, xh, sums, reach, adj, c1, c2, gain, taps, w_in):
    rows, span, d = x.shape
    t, h = c1.shape
    return call(
        functools.partial(gates_back_body, blocks),
        [((t, 2 * h), BF16), ((t, d), F32), ((8 * rows, d), F32), ((8, h), F32), ((8, d), F32)],
        (info, x, xh, sums, reach, adj, c1, c2, gain, taps, w_in),
        scratch=[pltpu.VMEM((span + 8, d), F32)] * 2,
        name="gates_back",
    )


def norm_back_body(x, gn, ret, gmid, gain, gx_o, gain_o):
    rows, span, d = x.shape
    total = jnp.zeros((1, d), F32)
    for r in range(rows):
        base = r * span
        xm = x[r].astype(F32)
        g = jnp.concatenate(
            [gn[base : base + span - 8, :], gn[base + span - 8 : base + span, :] + ret[8 * r : 8 * r + 8, :]], axis=0
        )
        rr = rms(xm)
        xhat = xm * rr
        total = total + jnp.sum(g * xhat, axis=0, keepdims=True)
        e = g * gain[0:1, :]
        gx = gmid[base : base + span, :] + rr * (e - xhat * jnp.mean(e * xhat, axis=-1, keepdims=True))
        gx_o[base : base + span, :] = gx.astype(gx_o.dtype)
    gain_o[...] = jnp.broadcast_to(total, gain_o.shape)


def norm_back(x, gn, ret, gmid, gain, kind):
    rows, span, d = x.shape
    return call(
        norm_back_body, [((rows * span, d), kind), ((8, d), F32)], (x, gn, ret, gmid, gain), scalars=0, name="norm_back"
    )


def pair_blocks(pairs):
    out = []
    for i, (left, right) in enumerate(pairs):
        d = 512
        for a in range(left.shape[1] // d):
            for b in range(right.shape[1] // d):
                out.append((i, a * d, b * d))
    return out


def part_body(blocks, rows, width, meta, *refs):
    out = refs[-1]
    for n, (i, a, b) in enumerate(blocks):
        left, right = refs[2 * i], refs[2 * i + 1]
        at = pl.multiple_of(a + meta[0] * rows, rows)
        out[:, n * width : (n + 1) * width] = dot(left[:, pl.ds(at, rows)], right[:, b : b + width], 0, 0).astype(BF16)


def sum_body(blocks, rows, width, meta, *refs):
    other, outs = refs[-5], refs[-4:]
    half = rows // 2
    cut = len(blocks) // 2
    for n, (i, a, b) in enumerate(blocks):
        left, right = refs[2 * i], refs[2 * i + 1]
        part = n // cut
        col = (n - part * cut) * width
        bit = meta[1 + part]
        for keep in range(2):
            take = bit if keep == 0 else 1 - bit
            at = pl.multiple_of(a + meta[0] * rows + take * half, half)
            got = other[pl.ds(pl.multiple_of(take * half, half), half), n * width : (n + 1) * width].astype(F32)
            outs[2 * part + keep][:, col : col + width] = (
                dot(left[:, pl.ds(at, half)], right[:, b : b + width], 0, 0) + got
            ).astype(BF16)


def group_sums(pairs, index, n, d):
    blocks = pair_blocks(pairs)
    flat = [m for pair in pairs for m in pair]
    width = d
    rows = d // 2
    wide = len(blocks) * width
    bit = lambda k: (index >> k) & 1
    sent = call(
        functools.partial(part_body, blocks, rows, width),
        [((rows, wide), BF16)],
        (jnp.stack([1 - bit(0)]), *flat),
        name="part",
    )[0]
    got = flip(sent, 0, n)
    half = ((rows // 2, wide // 2), BF16)
    return call(
        functools.partial(sum_body, blocks, rows, width),
        [half] * 4,
        (jnp.stack([bit(0), bit(2), bit(1)]), *flat, got),
        name="sum",
    )


def flip(value, bit, n):
    return lax.ppermute(value, AXES, [(i, i ^ (1 << bit)) for i in range(n)])


def halves(value, mine):
    h = value.shape[0] // 2
    return (
        lax.dynamic_slice_in_dim(value, mine * h, h, 0),
        lax.dynamic_slice_in_dim(value, (1 - mine) * h, h, 0),
    )


def add_low(a, b):
    return (a.astype(F32) + b.astype(F32)).astype(BF16)


def join(own, other, mine):
    first = mine == 0
    return jnp.concatenate([jnp.where(first, own, other), jnp.where(first, other, own)], 0)


def exchange(parts, index, n):
    bit = lambda k: (index >> k) & 1
    shards = []
    for p, (d1, d2) in enumerate(((2, 1), (1, 2))):
        keep, send = parts[2 * p], parts[2 * p + 1]
        got = flip(send, d1, n)
        k2, s2 = halves(keep, bit(d2))
        g2, h2 = halves(got, bit(d2))
        out = add_low(s2, h2)
        shards.append((add_low(k2, g2), flip(out, d2, n)))
    keep = jnp.concatenate([s[0] for s in shards], 1)
    got = jnp.concatenate([s[1] for s in shards], 1)
    for b in (3, 4):
        k2, s2 = halves(keep, bit(b))
        g2, h2 = halves(got, bit(b))
        out = add_low(s2, h2)
        keep, got = add_low(k2, g2), flip(out, b, n)
    total = add_low(keep, got)
    extra = 5
    while (1 << extra) < n:
        total = add_low(total, flip(total, extra, n))
        extra += 1
    for b in (4, 3):
        total = join(total, flip(total, b, n), bit(b))
    w = total.shape[1] // 2
    pieces = []
    for p, (d1, d2) in enumerate(((2, 1), (1, 2))):
        part = total[:, p * w : (p + 1) * w]
        part = join(part, flip(part, d2, n), bit(d2))
        far = flip(part, d1, n)
        pieces.append((part, far, flip(part, 0, n), flip(far, 0, n)))
    return pieces


def whole(pieces, index):
    bit = lambda k: (index >> k) & 1
    cols = []
    for p, d1 in enumerate((2, 1)):
        a, b, c, e = pieces[p]
        mine = join(a, b, bit(d1))
        theirs = join(c, e, bit(d1))
        cols.append(join(mine, theirs, bit(0)))
    return jnp.concatenate(cols, 1)


def passed_along(block, axis, distance):
    devices = range(lax.axis_size(axis))
    route = [(i - distance, i) for i in devices if i - distance in devices]
    return lax.ppermute(block, axis, route)


def shards(
    hidden_in, cotangent, lengths, norm_gain, conv_weight, gate_bias, in_weight, out_weight, up_weight, down_weight
):
    rows, span, d = hidden_in.shape
    layers = norm_gain.shape[0]
    h = gate_bias.shape[1]
    ff = up_weight.shape[2]
    kw = conv_weight.shape[1]
    blocks = lax.axis_size("blk")
    n = lax.axis_size("batch") * blocks
    block = lax.axis_index("blk")
    index = lax.axis_index("batch") * blocks + block
    starts = jnp.cumsum(lengths, axis=1, dtype=jnp.int32) - lengths
    info = jnp.concatenate([jnp.stack([block * span, block]).astype(jnp.int32), starts.reshape(-1)])

    x = hidden_in
    kept = []
    for l in range(layers):
        xh = passed_along(x[:, span - 8 :], "blk", 1)
        u, cand, c2, th, pa, conv, sums = gates(
            info, x, xh, norm_gain[l], conv_weight[l], gate_bias[l : l + 1], in_weight[l]
        )
        sums = lax.all_gather(sums, "blk", axis=0)
        state, c1, mid, sec, act, gp, out = mix(
            info, blocks, x, sums, th, pa, u, cand, norm_gain[l], out_weight[l], up_weight[l], down_weight[l]
        )
        kept.append((x, xh, u, c1, c2, conv, state, mid, sec, act, gp))
        x = out.reshape(rows, span, d)
    mixed = x.astype(BF16)

    g = cotangent.reshape(rows * span, d)
    big = [None] * layers
    small = [None] * layers
    for l in reversed(range(layers)):
        x, xh, u, c1, c2, conv, state, mid, sec, act, gp = kept[l]
        g_low, pre, gmid, branch, reach, adj, sums, gain_two = mlp_back(
            info, span, g, gp, mid, u, norm_gain[l], out_weight[l], up_weight[l], down_weight[l]
        )
        sums = lax.all_gather(sums, "blk", axis=0)
        proj, gn, ret, bias_sum, taps_sum = gates_back(
            info, blocks, x, xh, sums, reach, adj, c1, c2, norm_gain[l], conv_weight[l], in_weight[l]
        )
        ret = passed_along(ret, "blk", -1)
        g, gain_one = norm_back(x, gn, ret, gmid, norm_gain[l], F32 if l else BF16)
        parts = group_sums(((act, g_low), (sec, pre), (state, branch), (conv, proj)), index, n, d)
        big[l] = whole(exchange(parts, index, n), index).astype(F32)
        small[l] = (jnp.concatenate([gain_one[:1], gain_two[:1]], 0), taps_sum[:kw], bias_sum[0])
    input_grad = g.reshape(rows, span, d)

    def stacked(rows_of, first):
        return jnp.stack([rows_of(big[l][:, first:]) for l in range(layers)])

    def tall(count):
        return lambda m: m[:, : count * d].reshape(d, count, d).transpose(1, 0, 2).reshape(count * d, d)

    def flat(count):
        return lambda m: m[:, : count * d]

    first = (0, ff, 2 * ff, 2 * ff + h)
    g_down = stacked(tall(ff // d), first[0])
    g_up = stacked(flat(ff // d), first[1])
    g_out = stacked(tall(h // d), first[2])
    g_in = stacked(flat(2 * h // d), first[3])
    tiny = [jnp.stack([small[l][i] for l in range(layers)]) for i in range(3)]
    sizes = [m.size for m in tiny]
    line = lax.psum(jnp.concatenate([m.reshape(-1) for m in tiny]).reshape(-1, d), AXES).reshape(-1)
    g_gain = line[: sizes[0]].reshape(tiny[0].shape)
    g_conv = line[sizes[0] : sizes[0] + sizes[1]].reshape(tiny[1].shape)
    g_bias = line[sizes[0] + sizes[1] :].reshape(tiny[2].shape)
    return (mixed, input_grad, g_gain, g_conv, g_bias, g_in, g_out, g_up, g_down)


def solution(mesh):
    row = P("batch", "blk", None)
    return jax.shard_map(
        shards,
        mesh=mesh,
        in_specs=(row, row, P("batch", None)) + (P(),) * 7,
        out_specs=(row, row) + (P(),) * 7,
        check_vma=False,
    )
```

```python
import functools

import jax
import jax.numpy as jnp
from jax import lax
from jax.experimental import pallas as pl
from jax.experimental.pallas import tpu as pltpu
from jax.sharding import PartitionSpec as P

AXES = ("batch", "blk")
EPS = 1e-6
CHUNK = 256
STEP = 512
TINY = 128
F32 = jnp.float32
BF16 = jnp.bfloat16
MIB = 1024 * 1024
HBM = "hbm"
KEPT = "kept"


def call(body, outs, args, scratch=(), name=None, limit=8, aliases=None, cost=None):
    ins, specs = [], []
    for a in args:
        space = pltpu.VMEM
        if isinstance(a, tuple):
            if a[0] == HBM:
                space = pltpu.HBM
            a = pltpu.with_memory_space_constraint(a[1], space)
        specs.append(pl.BlockSpec(memory_space=space))
        ins.append(a)
    shapes, out_specs = [], []
    for o in outs:
        hbm = o[0] == HBM
        shape, kind = o[1:] if hbm else o
        shapes.append(pltpu.HBM(shape, kind) if hbm else jax.ShapeDtypeStruct(shape, kind))
        out_specs.append(pl.BlockSpec(memory_space=pltpu.HBM if hbm else pltpu.VMEM))
    return pl.pallas_call(
        body,
        out_shape=tuple(shapes),
        in_specs=specs,
        out_specs=tuple(out_specs),
        scratch_shapes=scratch,
        input_output_aliases=aliases or {},
        compiler_params=pltpu.CompilerParams(vmem_limit_bytes=limit * MIB),
        cost_estimate=cost,
        name=name,
    )(*ins)


def bit(k):
    index = lax.axis_index("batch") * lax.axis_size("blk") + lax.axis_index("blk")
    return (index >> k) & 1


def rows_at(which, count):
    return pl.ds(pl.multiple_of(which * count, count), count)


def dot(a, b, ca=1, cb=0):
    return lax.dot_general(a, b, (((ca,), (cb,)), ((), ())), preferred_element_type=F32)


def fetch(src, dst, sem):
    copy = pltpu.make_async_copy(src, dst, sem)
    copy.start()
    return copy


def offsets_of(lengths, row, span):
    docs = lengths.shape[1]
    pos = lax.axis_index("blk") * span + lax.broadcasted_iota(jnp.int32, (span, 1), 0)
    latest = jnp.zeros((span, 1), jnp.int32)
    start = lengths[row, 0]
    for j in range(1, docs):
        latest = jnp.where(start <= pos, start, latest)
        if j + 1 < docs:
            start = start + lengths[row, j]
    return pos - latest


def rms(values):
    return lax.rsqrt(jnp.mean(values * values, axis=-1, keepdims=True) + EPS)


def low(values):
    return values.astype(BF16).astype(F32)


def scan_forward(a, b, put):
    span, cols = a.shape
    a3, b3 = a.reshape(span // 8, 8, cols), b.reshape(span // 8, 8, cols)
    place = lax.broadcasted_iota(jnp.int32, (1, 8, cols), 1)
    for s in (1, 2, 4):
        inside = place >= s
        a_prev = jnp.where(inside, pltpu.roll(a3, s, 1), 1.0)
        b_prev = jnp.where(inside, pltpu.roll(b3, s, 1), 0.0)
        b3 = b3 + a3 * b_prev
        a3 = a3 * a_prev
    through = jnp.ones((1, cols), F32)
    state = jnp.zeros((1, cols), F32)
    for g in range(span // 8):
        st = b3[g] + a3[g] * state
        th = a3[g] * through
        put(8 * g, th, st)
        through, state = th[7:8], st[7:8]
    return through, state


def scan_backward(a, g, put):
    span, cols = a.shape
    b = a * g
    a3, b3 = a.reshape(span // 8, 8, cols), b.reshape(span // 8, 8, cols)
    place = lax.broadcasted_iota(jnp.int32, (1, 8, cols), 1)
    for s in (1, 2, 4):
        inside = place < 8 - s
        a_next = jnp.where(inside, pltpu.roll(a3, 8 - s, 1), 1.0)
        b_next = jnp.where(inside, pltpu.roll(b3, 8 - s, 1), 0.0)
        b3 = b3 + a3 * b_next
        a3 = a3 * a_next
    last = lax.broadcasted_iota(jnp.int32, (8, cols), 0) == 7
    reach = jnp.ones((1, cols), F32)
    value = jnp.zeros((1, cols), F32)
    for i in reversed(range(span // 8)):
        va = b3[i] + a3[i] * value
        re = a3[i] * reach
        put(8 * i, jnp.where(last, reach, pltpu.roll(re, 7, 0)), jnp.where(last, value, pltpu.roll(va, 7, 0)))
        reach, value = re[0:1], va[0:1]
    return reach, value


def entering(sums, me, row, lo, hi, forward):
    blocks = len(sums)
    enter = jnp.zeros((1, hi - lo), F32)
    for i in range(blocks - 1) if forward else reversed(range(1, blocks)):
        far = me ^ i
        factor, value = sums[1][2 * row : 2 * row + 1, lo:hi], sums[1][2 * row + 1 : 2 * row + 2, lo:hi]
        for k in range(2, blocks):
            factor = jnp.where(far == k, sums[k][2 * row : 2 * row + 1, lo:hi], factor)
            value = jnp.where(far == k, sums[k][2 * row + 1 : 2 * row + 2, lo:hi], value)
        enter = jnp.where(i < me if forward else i > me, factor * enter + value, enter)
    return enter


def gates_part(l, x, xh, gain, taps, bias, masks, w_in, arrived, u_o, cand_o, c2_o, th_o, pa_o, conv_o, sum_o, ext):
    rows, span, _ = x.shape
    hidden = u_o.shape[1]
    kw = taps.shape[1]
    g0 = gain[l, 0:1, :]
    for r in range(rows):
        base = r * span
        xm = x[r].astype(F32)
        ext[8 : 8 + span, :] = low(xm * rms(xm) * g0)
        xv = xh[r].astype(F32)
        ext[0:8, :] = low(xv * rms(xv) * g0)
        acc = taps[l, 0:1, :] * ext[8 : 8 + span, :]
        for k in range(1, kw):
            acc = acc + taps[l, k : k + 1, :] * ext[8 - k : 8 - k + span, :] * masks[base : base + span, k : k + 1]
        conv_o[base : base + span, :] = acc.astype(BF16)
    conv = conv_o[...]
    arrived()
    for c in range(hidden // CHUNK):
        lo, hi = c * CHUNK, (c + 1) * CHUNK
        pu = dot(conv, w_in[l, :, lo:hi]) + bias[l : l + 1, lo:hi]
        pc = dot(conv, w_in[l, :, hidden + lo : hidden + hi])
        u = jax.nn.sigmoid(pu)
        sg = jax.nn.sigmoid(pc)
        up = pc >= 0
        cand = jnp.where(up, pc + 0.5, sg)
        u_o[:, lo:hi] = u
        cand_o[:, lo:hi] = cand
        c2_o[:, lo:hi] = (u * jnp.where(up, 1.0, sg * (1.0 - sg))).astype(c2_o.dtype)
        b = u * cand
        for r in range(rows):
            base = r * span

            def put(row, th, st, base=base, lo=lo, hi=hi):
                th_o[base + row : base + row + 8, lo:hi] = th
                pa_o[base + row : base + row + 8, lo:hi] = st

            th, st = scan_forward((1.0 - u[base : base + span]) * masks[base : base + span, 1:2], b[base : base + span], put)
            sum_o[2 * r : 2 * r + 1, lo:hi] = th
            sum_o[2 * r + 1 : 2 * r + 2, lo:hi] = st


def gates_outs(rows, span, d, h):
    t = rows * span
    return [((t, h), F32), ((t, h), F32), ((t, h), BF16), ((t, h), F32), ((t, h), F32), ((t, d), BF16), ((2 * rows, h), F32)]


def first_gates_body(
    x_h, len_h, gain_h, taps_h, bias_h, xh, w_in,
    u_o, cand_o, c2_o, th_o, pa_o, conv_o, sum_o, x, gain, taps, bias, masks, ext, lengths, sem,
):
    pairs = ((len_h, lengths), (x_h, x), (gain_h, gain), (taps_h, taps), (bias_h, bias))
    copies = [fetch(src, dst, sem.at[i]) for i, (src, dst) in enumerate(pairs)]
    rows, span, _ = x.shape
    copies[0].wait()
    for r in range(rows):
        off = offsets_of(lengths, r, span)
        masks[r * span : (r + 1) * span, :] = (off >= lax.broadcasted_iota(jnp.int32, (span, 8), 1)).astype(F32)
    for copy in copies[1:]:
        copy.wait()
    gates_part(0, x, xh, gain, taps, bias, masks, w_in, lambda: None, u_o, cand_o, c2_o, th_o, pa_o, conv_o, sum_o, ext)


def first_gates(x, lengths, xh, gain, taps, bias, w_in):
    rows, span, d = x.shape
    h = bias.shape[1]
    return call(
        first_gates_body,
        gates_outs(rows, span, d, h)
        + [(x.shape, x.dtype), (gain.shape, F32), (taps.shape, F32), (bias.shape, F32), ((rows * span, 8), F32)],
        ((HBM, x), (HBM, lengths), (HBM, gain), (HBM, taps), (HBM, bias), xh, (KEPT, w_in)),
        scratch=[pltpu.VMEM((span + 8, d), F32), pltpu.SMEM(lengths.shape, jnp.int32), pltpu.SemaphoreType.DMA((5,))],
        name="first_gates",
    )


def gates_body(l, x, xh, gain, taps, bias, masks, w_in, *outs):
    gates_part(l, x, xh, gain, taps, bias, masks, w_in, lambda: None, *outs)


def gates(l, x, xh, gain, taps, bias, masks, w_in):
    rows, span, d = x.shape
    h = bias.shape[1]
    return call(
        functools.partial(gates_body, l),
        gates_outs(rows, span, d, h),
        (x, xh, gain, taps, bias, masks, (KEPT, w_in)),
        scratch=[pltpu.VMEM((span + 8, d), F32)],
        name="gates",
    )


def mix_part(l, x, sums, th, pa, u, cand, gain, masks, w_out, w_up, w_down, state_o, c1_o, mid_o, sec_o, act_o, gp_o):
    rows, span, _ = x.shape
    hidden = th.shape[1]
    ff = act_o.shape[1]
    me = lax.axis_index("blk")
    first = lax.broadcasted_iota(jnp.int32, (span, CHUNK), 0) == 0
    for c in range(hidden // CHUNK):
        lo, hi = c * CHUNK, (c + 1) * CHUNK
        for r in range(rows):
            base = r * span
            enter = entering(sums, me, r, lo, hi, True)
            st = pa[base : base + span, lo:hi] + th[base : base + span, lo:hi] * enter
            prev = jnp.where(first, enter, pltpu.roll(st, 1, 0))
            uu = u[base : base + span, lo:hi]
            alive = masks[base : base + span, 1:2]
            c1_o[base : base + span, lo:hi] = ((cand[base : base + span, lo:hi] - alive * prev) * uu * (1.0 - uu)).astype(c1_o.dtype)
            state_o[base : base + span, lo:hi] = st.astype(BF16)
    xs = jnp.concatenate([x[r].astype(F32) for r in range(rows)], axis=0)
    m = xs + dot(state_o[...], w_out[l])
    mid_o[...] = m
    sec = (m * rms(m) * gain[l, 1:2, :]).astype(BF16)
    sec_o[...] = sec
    out = m
    for c in range(ff // STEP):
        lo, hi = c * STEP, (c + 1) * STEP
        v = dot(sec, w_up[l, :, lo:hi])
        half = 0.5 * (1.0 + lax.erf(v * 0.7071067811865476))
        act = (v * half).astype(BF16)
        act_o[:, lo:hi] = act
        gp_o[:, lo:hi] = (half + v * (0.3989422804014327 * jnp.exp(-0.5 * v * v))).astype(gp_o.dtype)
        out = out + dot(act, w_down[l, lo:hi, :])
    return out


def mix_body(l, blocks, x, *refs):
    sums = refs[:blocks]
    th, pa, u, cand, gain, masks, wo, wu, wd, state_o, c1_o, mid_o, sec_o, act_o, gp_o, out_o, edge_o = refs[blocks:]
    out = mix_part(l, x, sums, th, pa, u, cand, gain, masks, wo, wu, wd, state_o, c1_o, mid_o, sec_o, act_o, gp_o)
    out = out.reshape(out_o.shape)
    out_o[...] = out
    edge_o[...] = out[:, out.shape[1] - 8 :, :]


def mix(l, x, sums, th, pa, u, cand, gain, masks, w_out, w_up, w_down):
    rows, span, d = x.shape
    t, h = th.shape
    ff = w_up.shape[2]
    return call(
        functools.partial(mix_body, l, len(sums)),
        [
            ((t, h), BF16), ((t, h), BF16), ((t, d), F32), ((t, d), BF16), ((t, ff), BF16), ((t, ff), BF16),
            ((rows, span, d), F32), ((rows, 8, d), F32),
        ],
        (x, *sums, th, pa, u, cand, gain, masks, (KEPT, w_out), (KEPT, w_up), (KEPT, w_down)),
        name="mix",
    )


def mlp_back_part(
    l, span, gf, gl, gp, mid, u, gain, masks, w_out, w_up, w_down, pre_o, gmid_o, branch_o, reach_o, adj_o, sum_o, gain_o
):
    hidden = u.shape[1]
    ff = pre_o.shape[1]
    rows = gf.shape[0] // span
    gs = jnp.zeros(gf.shape, F32)
    for c in range(ff // STEP):
        lo, hi = c * STEP, (c + 1) * STEP
        pre = (dot(gl, w_down[l, lo:hi, :], 1, 1) * gp[:, lo:hi].astype(F32)).astype(BF16)
        pre_o[:, lo:hi] = pre
        gs = gs + dot(pre, w_up[l, :, lo:hi], 1, 1)
    m = mid[...]
    rr = rms(m)
    xhat = m * rr
    gain_o[...] = jnp.broadcast_to(jnp.sum(gs * xhat, axis=0, keepdims=True), gain_o.shape)
    e = gs * gain[l, 1:2, :]
    gm = gf + rr * (e - xhat * jnp.mean(e * xhat, axis=-1, keepdims=True))
    gmid_o[...] = gm
    branch = gm.astype(BF16)
    branch_o[...] = branch
    for c in range(hidden // CHUNK):
        lo, hi = c * CHUNK, (c + 1) * CHUNK
        gstate = dot(branch, w_out[l, lo:hi, :], 1, 1)
        for r in range(rows):
            base = r * span
            gst = gstate[base : base + span]

            def put(row, re, va, base=base, lo=lo, hi=hi, gst=gst):
                reach_o[base + row : base + row + 8, lo:hi] = re
                adj_o[base + row : base + row + 8, lo:hi] = gst[row : row + 8] + va

            re, va = scan_backward((1.0 - u[base : base + span, lo:hi]) * masks[base : base + span, 1:2], gst, put)
            sum_o[2 * r : 2 * r + 1, lo:hi] = re
            sum_o[2 * r + 1 : 2 * r + 2, lo:hi] = va


def turn_body(l, blocks, x, *refs):
    sums = refs[:blocks]
    (
        th, pa, u, cand, g, gain, masks, wo, wu, wd,
        state_o, c1_o, sec_o, act_o, mixed_o, pre_o, gmid_o, branch_o, reach_o, adj_o, sum_o, gain_o, mid, gp,
    ) = refs[blocks:]
    span = x.shape[1]
    out = mix_part(l, x, sums, th, pa, u, cand, gain, masks, wo, wu, wd, state_o, c1_o, mid, sec_o, act_o, gp)
    mixed_o[...] = out.astype(BF16).reshape(mixed_o.shape)
    gl = g[...]
    mlp_back_part(
        l, span, gl.astype(F32), gl, gp, mid, u, gain, masks, wo, wu, wd, pre_o, gmid_o, branch_o, reach_o, adj_o, sum_o, gain_o
    )


def turn(l, x, sums, th, pa, u, cand, g, gain, masks, w_out, w_up, w_down):
    rows, span, d = x.shape
    t, h = th.shape
    ff = w_up.shape[2]
    return call(
        functools.partial(turn_body, l, len(sums)),
        [
            ((t, h), BF16), ((t, h), BF16), ((t, d), BF16), ((t, ff), BF16), ((rows, span, d), BF16),
            ((t, ff), BF16), ((t, d), F32), ((t, d), BF16), ((t, h), F32), ((t, h), F32), ((2 * rows, h), F32), ((8, d), F32),
        ],
        (x, *sums, th, pa, u, cand, g, gain, masks, (KEPT, w_out), (KEPT, w_up), (KEPT, w_down)),
        scratch=[pltpu.VMEM((t, d), F32), pltpu.VMEM((t, ff), F32)],
        name="turn",
    )


def norm_back_part(x, gn, ret, gmid, gain):
    rows, span, _ = x.shape
    out = []
    for r in range(rows):
        base = r * span
        xm = x[r].astype(F32)
        g = jnp.concatenate(
            [gn[base : base + span - 8, :], gn[base + span - 8 : base + span, :] + ret[8 * r : 8 * r + 8, :]], axis=0
        )
        rr = rms(xm)
        xhat = xm * rr
        e = g * gain
        out.append(gmid[base : base + span, :] + rr * (e - xhat * jnp.mean(e * xhat, axis=-1, keepdims=True)))
    return jnp.concatenate(out, axis=0)


def between_body(
    l, x_next, gn, ret, gmid, gp, mid, u, gain, masks, wo, wu, wd,
    low_o, pre_o, gmid_o, branch_o, reach_o, adj_o, sum_o, gain_o,
):
    g = norm_back_part(x_next, gn, ret, gmid, gain[l + 1, 0:1, :])
    gl = g.astype(BF16)
    low_o[...] = gl
    mlp_back_part(
        l, x_next.shape[1], g, gl, gp, mid, u, gain, masks, wo, wu, wd, pre_o, gmid_o, branch_o, reach_o, adj_o, sum_o, gain_o
    )


def between(l, x_next, gn, ret, gmid, gp, mid, u, gain, masks, w_out, w_up, w_down):
    t, d = mid.shape
    rows = x_next.shape[0]
    h, ff = u.shape[1], gp.shape[1]
    return call(
        functools.partial(between_body, l),
        [
            ((t, d), BF16), ((t, ff), BF16), ((t, d), F32), ((t, d), BF16), ((t, h), F32), ((t, h), F32), ((2 * rows, h), F32),
            ((8, d), F32),
        ],
        (x_next, gn, ret, gmid, gp, mid, u, gain, masks, (KEPT, w_out), (KEPT, w_up), (KEPT, w_down)),
        name="between",
    )


def gates_back_body(l, blocks, *refs):
    x, xh = refs[:2]
    sums = refs[2 : 2 + blocks]
    reach, adj, c1, c2, gain_two, gain, taps, masks, w_in, proj_o, gn_o, ret_o, tiny_o, ext, gext, small = refs[2 + blocks :]
    rows, span, d = x.shape
    hidden = c1.shape[1]
    kw = taps.shape[1]
    me = lax.axis_index("blk")
    small[...] = jnp.zeros(small.shape, F32)
    small[1:2, :] = gain_two[0:1, :]
    for c in range(hidden // CHUNK):
        lo, hi = c * CHUNK, (c + 1) * CHUNK
        total = jnp.zeros((1, CHUNK), F32)
        for r in range(rows):
            base = r * span
            enter = entering(sums, me, r, lo, hi, False)
            ad = adj[base : base + span, lo:hi] + reach[base : base + span, lo:hi] * enter
            gl = ad * c1[base : base + span, lo:hi].astype(F32)
            total = total + jnp.sum(gl, axis=0, keepdims=True)
            proj_o[base : base + span, lo:hi] = gl.astype(BF16)
            proj_o[base : base + span, hidden + lo : hidden + hi] = (ad * c2[base : base + span, lo:hi].astype(F32)).astype(BF16)
        at = 2 + kw + lo // d
        small[at : at + 1, lo % d : lo % d + CHUNK] = total
    gci = dot(proj_o[...], w_in[l], 1, 1)
    g0 = gain[l, 0:1, :]
    for r in range(rows):
        base = r * span
        xm = x[r].astype(F32)
        xhat = xm * rms(xm)
        ext[8 : 8 + span, :] = low(xhat * g0)
        xv = xh[r].astype(F32)
        xhat_h = xv * rms(xv)
        ext[0:8, :] = low(xhat_h * g0)
        gr = gci[base : base + span]
        gext[0:8, :] = jnp.zeros((8, d), F32)
        gext[8 : 8 + span, :] = gr * taps[l, 0:1, :]
        small[2:3, :] += jnp.sum(gr * ext[8 : 8 + span, :], axis=0, keepdims=True)
        for k in range(1, kw):
            gk = gr * masks[base : base + span, k : k + 1]
            small[2 + k : 3 + k, :] += jnp.sum(gk * ext[8 - k : 8 - k + span, :], axis=0, keepdims=True)
            gext[8 - k : 8 - k + span, :] = gext[8 - k : 8 - k + span, :] + gk * taps[l, k : k + 1, :]
        own, back = gext[8 : 8 + span, :], gext[0:8, :]
        small[0:1, :] += jnp.sum(own * xhat, axis=0, keepdims=True) + jnp.sum(back * xhat_h, axis=0, keepdims=True)
        gn_o[base : base + span, :] = own
        ret_o[8 * r : 8 * r + 8, :] = back
    for q in range(d // TINY):
        tiny_o[8 * q : 8 * q + 8, :] = small[:, q * TINY : (q + 1) * TINY]


def gates_back(l, x, xh, sums, reach, adj, c1, c2, gain_two, gain, taps, masks, w_in):
    rows, span, d = x.shape
    t, h = c1.shape
    return call(
        functools.partial(gates_back_body, l, len(sums)),
        [((t, 2 * h), BF16), ((t, d), F32), ((8 * rows, d), F32), ((8 * d // TINY, TINY), F32)],
        (x, xh, *sums, reach, adj, c1, c2, gain_two, gain, taps, masks, (KEPT, w_in)),
        scratch=[pltpu.VMEM((span + 8, d), F32)] * 2 + [pltpu.VMEM((8, d), F32)],
        name="gates_back",
    )


def norm_back_body(x, gn, ret, gmid, gain, gx_o):
    gx_o[...] = norm_back_part(x, gn, ret, gmid, gain[0, 0:1, :]).astype(gx_o.dtype).reshape(gx_o.shape)


def norm_back(x, gn, ret, gmid, gain):
    return call(norm_back_body, [(x.shape, BF16)], (x, gn, ret, gmid, gain), name="norm_back")[0]


def blocks_of(pairs, d):
    return [
        (i, a, b) for i, (left, right) in enumerate(pairs) for a in range(0, left.shape[1], d) for b in range(0, right.shape[1], d)
    ]


def part_body(blocks, d, tiny_rows, *refs):
    out = refs[-1]
    rows = out.shape[0]
    other = 1 - bit(0)
    for n, (i, a, b) in enumerate(blocks):
        at = pl.multiple_of(a + other * rows, rows)
        out[:, n * d : (n + 1) * d] = dot(refs[2 * i][:, pl.ds(at, rows)], refs[2 * i + 1][:, b : b + d], 0, 0).astype(BF16)
    if tiny_rows:
        lo = len(blocks) * d
        out[:, lo:] = jnp.zeros((rows, TINY), BF16)
        out[0:tiny_rows, lo:] = (refs[-2][...] * (other == 0).astype(F32)).astype(BF16)


def sum_body(blocks, d, tiny_rows, *refs):
    other, outs = refs[-5], refs[-4:]
    rows = other.shape[0]
    half = rows // 2
    cut = len(blocks) // 2
    core = bit(0)
    for part in range(2):
        mine = bit(2 - part)
        for keep in (1, 0):
            take = mine if keep == 0 else 1 - mine
            here = rows_at(take, half)
            out = outs[2 * part + keep]
            for n in range(part * cut, (part + 1) * cut):
                i, a, b = blocks[n]
                at = pl.multiple_of(a + core * rows + take * half, half)
                got = other[here, n * d : (n + 1) * d].astype(F32)
                col = (n - part * cut) * d
                out[:, col : col + d] = (dot(refs[2 * i][:, pl.ds(at, half)], refs[2 * i + 1][:, b : b + d], 0, 0) + got).astype(BF16)
            if tiny_rows and part == 1:
                lo, col = len(blocks) * d, cut * d
                out[:, col:] = other[here, lo:]
                here0 = jnp.logical_and(core == 0, take == 0).astype(F32)
                out[0:tiny_rows, col:] = (
                    other[pl.ds(pl.multiple_of(take * half, half), tiny_rows), lo:].astype(F32) + refs[-6][...] * here0
                ).astype(BF16)


def part(pairs, tiny, d):
    blocks = blocks_of(pairs, d)
    flat = [m for pair in pairs for m in pair] + ([tiny] if tiny is not None else [])
    wide = len(blocks) * d + (0 if tiny is None else TINY)
    body = functools.partial(part_body, blocks, d, 0 if tiny is None else tiny.shape[0])
    return call(body, [((d // 2, wide), BF16)], flat, name="part")[0]


def group_sums(pairs, tiny, got, d):
    blocks = blocks_of(pairs, d)
    flat = [m for pair in pairs for m in pair] + ([tiny] if tiny is not None else [])
    extra = 0 if tiny is None else TINY
    first = ((d // 4, len(blocks) * d // 2), BF16)
    second = ((d // 4, len(blocks) * d // 2 + extra), BF16)
    body = functools.partial(sum_body, blocks, d, 0 if tiny is None else tiny.shape[0])
    return call(body, [first, first, second, second], (*flat, got), name="sum")


def flip(value, k, n):
    return lax.ppermute(value, AXES, [(i, i ^ (1 << k)) for i in range(n)])


def add_rows(keep, got, where):
    return (keep[where, :].astype(F32) + got[where, :].astype(F32)).astype(BF16)


def add_body(k, keep, got, keep_o, send_o):
    half = keep_o.shape[0]
    mine = bit(k)
    send_o[...] = add_rows(keep, got, rows_at(1 - mine, half))
    keep_o[...] = add_rows(keep, got, rows_at(mine, half))


def add_split(keep, got, k):
    shape = (keep.shape[0] // 2, keep.shape[1])
    return call(functools.partial(add_body, k), [(shape, BF16)] * 2, (keep, got), name="add", limit=4)


def add_both_body(k, keep_a, got_a, keep_b, got_b, keep_o, send_o):
    half = keep_o.shape[0]
    cut = keep_a.shape[1]
    mine = bit(k)
    for out, which in ((send_o, 1 - mine), (keep_o, mine)):
        out[:, :cut] = add_rows(keep_a, got_a, rows_at(which, half))
        out[:, cut:] = add_rows(keep_b, got_b, rows_at(which, half))


def add_both(keep_a, got_a, keep_b, got_b, k):
    shape = (keep_a.shape[0] // 2, keep_a.shape[1] + keep_b.shape[1])
    return call(functools.partial(add_both_body, k), [(shape, BF16)] * 2, (keep_a, got_a, keep_b, got_b), name="add_both", limit=4)


def add_whole_body(keep, got, out):
    out[...] = add_rows(keep, got, slice(None))


def add_whole(keep, got):
    return call(add_whole_body, [(keep.shape, BF16)], (keep, got), name="add_whole", limit=4)[0]


def join_body(k, own, other, *outs):
    rows = own.shape[0]
    mine = bit(k)
    lo = 0
    for out in outs:
        hi = lo + out.shape[1]
        out[rows_at(mine, rows), :] = own[:, lo:hi]
        out[rows_at(1 - mine, rows), :] = other[:, lo:hi]
        lo = hi


def join(own, other, k, cut=None):
    rows, cols = own.shape
    widths = [cols] if cut is None else [cut, cols - cut]
    return call(functools.partial(join_body, k), [((2 * rows, w), BF16) for w in widths], (own, other), name="join", limit=4)


def reduce_rest(parts, n):
    shards = []
    for p, (d1, d2) in enumerate(((2, 1), (1, 2))):
        keep, send = add_split(parts[2 * p], flip(parts[2 * p + 1], d1, n), d2)
        shards += [keep, flip(send, d2, n)]
    keep, send = add_both(*shards, 3)
    keep, send = add_split(keep, flip(send, 3, n), 4)
    total = add_whole(keep, flip(send, 4, n))
    k = 5
    while (1 << k) < n:
        total = add_whole(total, flip(total, k, n))
        k += 1
    return total


def gather_rest(total, cut, n):
    (total,) = join(total, flip(total, 4, n), 4)
    halves = join(total, flip(total, 3, n), 3, cut)
    pieces = []
    for own, (d1, d2) in zip(halves, ((2, 1), (1, 2))):
        (own,) = join(own, flip(own, d2, n), d2)
        far = flip(own, d1, n)
        pieces += [own, far, flip(own, 0, n), flip(far, 0, n)]
    return pieces


SLOTS = 8


def spread_body(l, places, d, tiny_rows, count, aliased, *refs):
    pieces = refs[:8]
    at = 8 + aliased
    tiny_in = refs[at] if tiny_rows == 2 else None
    at += 1 if tiny_rows == 2 else 0
    outs = refs[at : at + count]
    tiny_outs = refs[at + count : -3] if tiny_rows else ()
    stage, tiny_all, sem = refs[-3:]
    rows = pieces[0].shape[0]
    cut = len(places) // 2
    flying = [None] * SLOTS
    step = 0
    for part in range(2):
        for k in range(4):
            piece = pieces[4 * part + k]
            core = bit(0) if k < 2 else 1 - bit(0)
            side = bit(2 - part) if k % 2 == 0 else 1 - bit(2 - part)
            row = core * (2 * rows) + side * rows
            for n in range(part * cut, (part + 1) * cut):
                out, r, c = places[n]
                slot = step % SLOTS
                if flying[slot] is not None:
                    flying[slot].wait()
                col = (n - part * cut) * d
                stage[slot] = piece[:, col : col + d].astype(F32)
                there = outs[out].at[l, pl.ds(pl.multiple_of(r + row, rows), rows), pl.ds(c, d)]
                flying[slot] = fetch(stage.at[slot], there, sem.at[slot])
                step += 1
            if tiny_rows and part == 1:
                tiny_all[pl.ds(pl.multiple_of(row, rows), rows), :] = piece[:, cut * d :].astype(F32)
    if tiny_rows == 1:
        for q in range(d // TINY):
            tiny_outs[0][:, q * TINY : (q + 1) * TINY] = tiny_all[8 * q : 8 * q + 8, :]
    if tiny_rows == 2:
        gain_o, taps_o, bias_o = tiny_outs
        kw = taps_o.shape[1]
        for q in range(d // TINY):
            lo, hi = q * TINY, (q + 1) * TINY
            for layer in range(2):
                own = tiny_all[8 * q : 8 * q + 8, :] if layer == 0 else tiny_in[:, lo:hi]
                gain_o[layer, :, lo:hi] = own[0:2]
                taps_o[layer, :, lo:hi] = own[2 : 2 + kw]
                for b in range(bias_o.shape[1] // d):
                    bias_o[layer : layer + 1, b * d + lo : b * d + hi] = own[2 + kw + b : 3 + kw + b]
    for copy in flying:
        if copy is not None:
            copy.wait()


def spread(l, pieces, places, shapes, old, tiny_in, tiny_kind, tiny_shapes, d):
    args = [*pieces]
    aliases = {}
    if old is not None:
        for i, o in enumerate(old):
            aliases[len(args)] = i
            args.append((HBM, o))
    if tiny_kind == 2:
        args.append(tiny_in)
    rows = pieces[0].shape[0]
    return call(
        functools.partial(spread_body, l, places, d, tiny_kind, len(shapes), len(old) if old is not None else 0),
        [(HBM, s, F32) for s in shapes] + [(s, F32) for s in tiny_shapes],
        args,
        scratch=[
            pltpu.VMEM((SLOTS, rows, d), F32),
            pltpu.VMEM((4 * rows, TINY), F32),
            pltpu.SemaphoreType.DMA((SLOTS,)),
        ],
        aliases=aliases,
        name="spread",
    )


def passed_along(block, axis, distance):
    devices = range(lax.axis_size(axis))
    route = [(i - distance, i) for i in devices if i - distance in devices]
    return lax.ppermute(block, axis, route)


def from_blocks(value):
    size = lax.axis_size("blk")
    got = {0: value}
    far = size >> 1
    while far:
        for k, v in list(got.items()):
            got[k | far] = lax.ppermute(v, "blk", [(i, i ^ far) for i in range(size)])
        far >>= 1
    return [got[k] for k in range(size)]


def shards(
    hidden_in, cotangent, lengths, norm_gain, conv_weight, gate_bias, in_weight, out_weight, up_weight, down_weight
):
    rows, span, d = hidden_in.shape
    h = gate_bias.shape[1]
    ff = up_weight.shape[2]
    blocks = lax.axis_size("blk")
    n = lax.axis_size("batch") * blocks
    mlp = (out_weight, up_weight, down_weight)
    forth = lambda edge: passed_along(edge, "blk", 1)
    back = lambda edge: passed_along(edge, "blk", -1)

    xh0 = forth(hidden_in[:, span - 8 :])
    u0, cand, c20, th, pa, conv0, sums, x0, gain, taps, bias, masks = first_gates(
        hidden_in, lengths, xh0, norm_gain, conv_weight, gate_bias, in_weight
    )
    state0, c10, mid0, sec0, act0, gp0, x1, edge = mix(0, x0, from_blocks(sums), th, pa, u0, cand, gain, masks, *mlp)
    xh1 = forth(edge)
    u1, cand, c21, th, pa, conv1, sums = gates(1, x1, xh1, gain, taps, bias, masks, in_weight)
    g = cotangent.reshape(rows * span, d)
    state1, c11, sec1, act1, mixed, pre1, gmid1, branch1, reach, adj, sums, gain_two = turn(
        1, x1, from_blocks(sums), th, pa, u1, cand, g, gain, masks, *mlp
    )
    pairs_a = ((act1, g), (sec1, pre1))
    got_a = flip(part(pairs_a, None, d), 0, n)
    proj1, gn, ret, tiny1 = gates_back(1, x1, xh1, from_blocks(sums), reach, adj, c11, c21, gain_two, gain, taps, masks, in_weight)
    ret = back(ret)
    pairs_b = ((state1, branch1), (conv1, proj1))
    got_b = flip(part(pairs_b, tiny1, d), 0, n)
    parts_a = group_sums(pairs_a, None, got_a, d)
    low0, pre0, gmid0, branch0, reach, adj, sums, gain_two = between(0, x1, gn, ret, gmid1, gp0, mid0, u0, gain, masks, *mlp)
    pairs_c = ((act0, low0), (sec0, pre0))
    got_c = flip(part(pairs_c, None, d), 0, n)
    parts_b = group_sums(pairs_b, tiny1, got_b, d)
    proj0, gn, ret, tiny0 = gates_back(0, x0, xh0, from_blocks(sums), reach, adj, c10, c20, gain_two, gain, taps, masks, in_weight)
    pairs_d = ((state0, branch0), (conv0, proj0))
    got_d = flip(part(pairs_d, tiny0, d), 0, n)
    parts_c = group_sums(pairs_c, None, got_c, d)
    parts_d = group_sums(pairs_d, tiny0, got_d, d)
    input_grad = norm_back(x0, gn, back(ret), gmid0, gain)
    pieces = [gather_rest(reduce_rest(p, n), p[0].shape[1], n) for p in (parts_a, parts_b, parts_c, parts_d)]

    first = [(0, j * d, 0) for j in range(ff // d)] + [(1, 0, j * d) for j in range(ff // d)]
    second = [(0, j * d, 0) for j in range(h // d)] + [(1, 0, j * d) for j in range(2 * h // d)]
    first_shapes = [down_weight.shape, up_weight.shape]
    second_shapes = [out_weight.shape, in_weight.shape]
    outs = spread(1, pieces[0], first, first_shapes, None, None, 0, [], d)
    *outs2, small1 = spread(1, pieces[1], second, second_shapes, None, None, 1, [(8, d)], d)
    g_down, g_up = spread(0, pieces[2], first, first_shapes, outs, None, 0, [], d)
    g_out, g_in, g_gain, g_conv, g_bias = spread(
        0, pieces[3], second, second_shapes, outs2, small1, 2, [norm_gain.shape, conv_weight.shape, gate_bias.shape], d
    )
    return (mixed, input_grad, g_gain, g_conv, g_bias, g_in, g_out, g_up, g_down)


def solution(mesh):
    row = P("batch", "blk", None)
    return jax.shard_map(
        shards,
        mesh=mesh,
        in_specs=(row, row, P("batch", None)) + (P(),) * 7,
        out_specs=(row, row) + (P(),) * 7,
        check_vma=False,
    )
```

```python
import functools

import jax
import jax.numpy as jnp
from jax import lax
from jax.experimental import pallas as pl
from jax.experimental.pallas import tpu as pltpu
from jax.sharding import PartitionSpec as P

AXES = ("batch", "blk")
EPS = 1e-6
CHUNK = 256
STEP = 512
TINY = 128
F32 = jnp.float32
BF16 = jnp.bfloat16
MIB = 1024 * 1024
HBM = "hbm"
KEPT = "kept"


def call(body, outs, args, scratch=(), name=None, limit=8, aliases=None, cost=None, waits=()):
    ins, specs = [], []
    for a in args:
        space = pltpu.VMEM
        if isinstance(a, tuple):
            if a[0] == HBM:
                space = pltpu.HBM
            a = pltpu.with_memory_space_constraint(a[1], space)
        specs.append(pl.BlockSpec(memory_space=space))
        ins.append(a)
    shapes, out_specs = [], []
    for o in outs:
        hbm = o[0] == HBM
        shape, kind = o[1:] if isinstance(o[0], str) else o
        shapes.append(pltpu.HBM(shape, kind) if hbm else pltpu.VMEM(shape, kind) if o[0] == KEPT else jax.ShapeDtypeStruct(shape, kind))
        out_specs.append(pl.BlockSpec(memory_space=pltpu.HBM if hbm else pltpu.VMEM))
    given = len(ins)
    for w in waits:
        specs.append(pl.BlockSpec(memory_space=pl.ANY))
        ins.append(w)

    def run(*refs):
        body(*refs[:given], *refs[len(ins) :])

    return pl.pallas_call(
        run if waits else body,
        out_shape=tuple(shapes),
        in_specs=specs,
        out_specs=tuple(out_specs),
        scratch_shapes=scratch,
        input_output_aliases=aliases or {},
        compiler_params=pltpu.CompilerParams(vmem_limit_bytes=limit * MIB),
        cost_estimate=cost,
        name=name,
    )(*ins)


def bit(k):
    index = lax.axis_index("batch") * lax.axis_size("blk") + lax.axis_index("blk")
    return (index >> k) & 1


def rows_at(which, count):
    return pl.ds(pl.multiple_of(which * count, count), count)


def dot(a, b, ca=1, cb=0):
    return lax.dot_general(a, b, (((ca,), (cb,)), ((), ())), preferred_element_type=F32)


def fetch(src, dst, sem):
    copy = pltpu.make_async_copy(src, dst, sem)
    copy.start()
    return copy


def offsets_of(lengths, row, span):
    docs = lengths.shape[1]
    pos = lax.axis_index("blk") * span + lax.broadcasted_iota(jnp.int32, (span + 8, 1), 0)
    latest = jnp.zeros((span + 8, 1), jnp.int32)
    start = lengths[row, 0]
    for j in range(1, docs):
        latest = jnp.where(start <= pos, start, latest)
        if j + 1 < docs:
            start = start + lengths[row, j]
    return pos - latest


def rms(values):
    return lax.rsqrt(jnp.mean(values * values, axis=-1, keepdims=True) + EPS)


def low(values):
    return values.astype(BF16).astype(F32)


def scan_forward(a, b, put):
    span, cols = a.shape
    a3, b3 = a.reshape(span // 8, 8, cols), b.reshape(span // 8, 8, cols)
    place = lax.broadcasted_iota(jnp.int32, (1, 8, cols), 1)
    for s in (1, 2, 4):
        inside = place >= s
        a_prev = jnp.where(inside, pltpu.roll(a3, s, 1), 1.0)
        b_prev = jnp.where(inside, pltpu.roll(b3, s, 1), 0.0)
        b3 = b3 + a3 * b_prev
        a3 = a3 * a_prev
    through = jnp.ones((1, cols), F32)
    state = jnp.zeros((1, cols), F32)
    for g in range(span // 8):
        st = b3[g] + a3[g] * state
        th = a3[g] * through
        put(8 * g, th, st)
        through, state = th[7:8], st[7:8]
    return through, state


def scan_backward(a, g, put):
    span, cols = a.shape
    b = a * g
    a3, b3 = a.reshape(span // 8, 8, cols), b.reshape(span // 8, 8, cols)
    place = lax.broadcasted_iota(jnp.int32, (1, 8, cols), 1)
    for s in (1, 2, 4):
        inside = place < 8 - s
        a_next = jnp.where(inside, pltpu.roll(a3, 8 - s, 1), 1.0)
        b_next = jnp.where(inside, pltpu.roll(b3, 8 - s, 1), 0.0)
        b3 = b3 + a3 * b_next
        a3 = a3 * a_next
    last = lax.broadcasted_iota(jnp.int32, (8, cols), 0) == 7
    reach = jnp.ones((1, cols), F32)
    value = jnp.zeros((1, cols), F32)
    for i in reversed(range(span // 8)):
        va = b3[i] + a3[i] * value
        re = a3[i] * reach
        put(8 * i, jnp.where(last, reach, pltpu.roll(re, 7, 0)), jnp.where(last, value, pltpu.roll(va, 7, 0)))
        reach, value = re[0:1], va[0:1]
    return reach, value


def from_block(sums, far, rows, lo, hi):
    value = sums[1][rows, lo:hi]
    for k in range(2, len(sums)):
        value = jnp.where(far == k, sums[k][rows, lo:hi], value)
    return value


def row_of(value, i):
    return value[i : i + 1]


def entering_forward(sums, row, lo, hi):
    me = lax.axis_index("blk")
    rows = slice(8 * row, 8 * row + 8)
    enter = jnp.zeros((1, hi - lo), F32)
    before = enter
    own = None
    for i in range(len(sums) - 1):
        got = from_block(sums, me ^ i, rows, lo, hi)
        before = jnp.where(i == me - 1, enter, before)
        own = got if own is None else jnp.where(i == me - 1, got, own)
        enter = jnp.where(i < me, row_of(got, 2) * enter + row_of(got, 5), enter)
    return enter, before, own


def entering_backward(sums, row, lo, hi):
    me = lax.axis_index("blk")
    rows = slice(16 * row, 16 * row + 16)
    enter = jnp.zeros((1, hi - lo), F32)
    after = enter
    own = None
    for i in reversed(range(1, len(sums))):
        got = from_block(sums, me ^ i, rows, lo, hi).astype(F32)
        after = jnp.where(i == me + 1, enter, after)
        own = got if own is None else jnp.where(i == me + 1, got, own)
        step = (row_of(got, 12) + row_of(got, 13)) * enter + (row_of(got, 14) + row_of(got, 15))
        enter = jnp.where(i > me, step, enter)
    return enter, after, own


def gates_part(l, x, xh, gain, taps, bias, masks, w_in, u_o, cand_o, c2_o, th_o, pa_o, conv_o, sum_o, ext):
    rows, span, _ = x.shape
    hidden = u_o.shape[1]
    kw = taps.shape[1]
    g0 = gain[l, 0:1, :]
    for r in range(rows):
        base = r * span
        xm = x[r].astype(F32)
        ext[8 : 8 + span, :] = low(xm * rms(xm) * g0)
        xv = xh[r].astype(F32)
        ext[0:8, :] = low(xv * rms(xv) * g0)
        acc = taps[l, 0:1, :] * ext[8 : 8 + span, :]
        for k in range(1, kw):
            acc = acc + taps[l, k : k + 1, :] * ext[8 - k : 8 - k + span, :] * masks[r, 0:span, k : k + 1]
        conv_o[base : base + span, :] = acc.astype(BF16)
    conv = conv_o[...]
    for c in range(hidden // CHUNK):
        lo, hi = c * CHUNK, (c + 1) * CHUNK
        pu = dot(conv, w_in[l, :, lo:hi]) + bias[l : l + 1, lo:hi]
        pc = dot(conv, w_in[l, :, hidden + lo : hidden + hi])
        u = jax.nn.sigmoid(pu)
        sg = jax.nn.sigmoid(pc)
        up = pc >= 0
        cand = jnp.where(up, pc + 0.5, sg)
        u_o[:, lo:hi] = u
        cand_o[:, lo:hi] = cand
        c2_o[:, lo:hi] = (u * jnp.where(up, 1.0, sg * (1.0 - sg))).astype(c2_o.dtype)
        b = u * cand
        for r in range(rows):
            base = r * span

            def put(row, th, st, base=base, lo=lo, hi=hi):
                th_o[base + row : base + row + 8, lo:hi] = th
                pa_o[base + row : base + row + 8, lo:hi] = st

            scan_forward((1.0 - u[base : base + span]) * masks[r, 0:span, 1:2], b[base : base + span], put)
            end = base + span
            sum_o[8 * r : 8 * r + 3, lo:hi] = th_o[end - 3 : end, lo:hi]
            sum_o[8 * r + 3 : 8 * r + 6, lo:hi] = pa_o[end - 3 : end, lo:hi]
            sum_o[8 * r + 6 : 8 * r + 8, lo:hi] = jnp.zeros((2, hi - lo), F32)


def gates_outs(rows, span, d, h):
    t = rows * span
    return [((t, h), F32), ((t, h), F32), ((t, h), BF16), ((t, h), F32), ((t, h), F32), ((t, d), BF16), ((8 * rows, h), F32)]


def load_body(x_h, len_h, gain_h, taps_h, bias_h, wi_h, *refs):
    x, gain, taps, bias, wi, masks, lengths, sem = refs
    pairs = ((len_h, lengths), (wi_h, wi), (x_h, x), (gain_h, gain), (taps_h, taps), (bias_h, bias))
    copies = [fetch(src, dst, sem.at[i]) for i, (src, dst) in enumerate(pairs)]
    rows, span, _ = x.shape
    copies[0].wait()
    for r in range(rows):
        off = offsets_of(lengths, r, span)
        masks[r] = (off >= lax.broadcasted_iota(jnp.int32, (span + 8, 8), 1)).astype(F32)
    for copy in copies[1:]:
        copy.wait()


def load(x, lengths, gain, taps, bias, w_in):
    rows, span, _ = x.shape
    kept = (x, gain, taps, bias, w_in)
    return call(
        load_body,
        [(KEPT, a.shape, a.dtype) for a in kept] + [(KEPT, (rows, span + 8, 8), F32)],
        [(HBM, a) for a in (x, lengths, gain, taps, bias, w_in)],
        scratch=[pltpu.SMEM(lengths.shape, jnp.int32), pltpu.SemaphoreType.DMA((6,))],
        name="load",
    )


def gates_body(l, x, xh, gain, taps, bias, masks, w_in, *refs):
    count = (len(refs) - 9) // 2
    sources, outs, targets, (ext, sem) = refs[:count], refs[count : count + 7], refs[count + 7 : -2], refs[-2:]
    copies = [fetch(src, dst, sem.at[i]) for i, (src, dst) in enumerate(zip(sources, targets))]
    gates_part(l, x, xh, gain, taps, bias, masks, w_in, *outs, ext)
    for copy in copies:
        copy.wait()


def gates(l, x, xh, gain, taps, bias, masks, w_in, weights):
    rows, span, d = x.shape
    h = bias.shape[1]
    return call(
        functools.partial(gates_body, l),
        gates_outs(rows, span, d, h) + [(KEPT, a.shape, a.dtype) for a in weights],
        (x, xh, gain, taps, bias, masks, w_in, *[(HBM, a) for a in weights]),
        scratch=[pltpu.VMEM((span + 8, d), F32), pltpu.SemaphoreType.DMA((len(weights),))],
        name="gates",
    )


def mix_part(l, x, xh, sums, th, pa, u, cand, gain, masks, w_out, w_up, w_down, state, c1_o, mid_o, sec_o, act_o, gp_o):
    rows, span, _ = x.shape
    t = rows * span
    hidden = th.shape[1]
    ff = act_o.shape[1]
    first = lax.broadcasted_iota(jnp.int32, (span, CHUNK), 0) == 0
    for c in range(hidden // CHUNK):
        lo, hi = c * CHUNK, (c + 1) * CHUNK
        halo = []
        for r in range(rows):
            base = r * span
            enter, before, edge = entering_forward(sums, r, lo, hi)
            st = pa[base : base + span, lo:hi] + th[base : base + span, lo:hi] * enter
            prev = jnp.where(first, enter, pltpu.roll(st, 1, 0))
            uu = u[base : base + span, lo:hi]
            alive = masks[r, 0:span, 1:2]
            c1_o[base : base + span, lo:hi] = ((cand[base : base + span, lo:hi] - alive * prev) * uu * (1.0 - uu)).astype(c1_o.dtype)
            state[base : base + span, lo:hi] = st.astype(BF16)
            halo.append(pltpu.roll(edge, 2, 0) + pltpu.roll(edge, 5, 0) * before)
        if xh is not None:
            state[t : t + 8 * rows, lo:hi] = jnp.concatenate(halo, axis=0).astype(BF16)
    xs = [x[r].astype(F32) for r in range(rows)]
    if xh is not None:
        xs += [xh[r].astype(F32) for r in range(rows)]
    m = jnp.concatenate(xs, axis=0) + dot(state[...], w_out[l])
    mid_o[...] = m[:t]
    sec = (m * rms(m) * gain[l, 1:2, :]).astype(BF16)
    sec_o[...] = sec[:t]
    out = m
    for c in range(ff // STEP):
        lo, hi = c * STEP, (c + 1) * STEP
        v = dot(sec, w_up[l, :, lo:hi])
        half = 0.5 * (1.0 + lax.erf(v * 0.7071067811865476))
        act = (v * half).astype(BF16)
        act_o[:, lo:hi] = act[:t]
        v, half = v[:t], half[:t]
        gp_o[:, lo:hi] = (half + v * (0.3989422804014327 * jnp.exp(-0.5 * v * v))).astype(gp_o.dtype)
        out = out + dot(act, w_down[l, lo:hi, :])
    return out


def middle_body(l, blocks, x, xh, *refs):
    sums = refs[:blocks]
    th, pa, u, cand, gain, taps, bias, masks, wi, wo, wu, wd = refs[blocks : blocks + 12]
    state_o, c1_o, mid_o, sec_o, act_o, gp_o, out_o, edge_o = refs[blocks + 12 : blocks + 20]
    gate_outs = refs[blocks + 20 : -2]
    ext, state = refs[-2:]
    rows, span, d = x.shape
    t = rows * span
    out = mix_part(l, x, xh, sums, th, pa, u, cand, gain, masks, wo, wu, wd, state, c1_o, mid_o, sec_o, act_o, gp_o)
    state_o[...] = state[0:t, :]
    out_o[...] = out[:t].reshape(rows, span, d)
    edge_o[...] = out[t:].reshape(rows, 8, d)
    gates_part(l + 1, out_o, edge_o, gain, taps, bias, masks, wi, *gate_outs, ext)


def middle(l, x, xh, sums, th, pa, u, cand, gain, taps, bias, masks, w_in, w_out, w_up, w_down):
    rows, span, d = x.shape
    t, h = th.shape
    ff = w_up.shape[2]
    return call(
        functools.partial(middle_body, l, len(sums)),
        [
            ((t, h), BF16), ((t, h), BF16), ((t, d), F32), ((t, d), BF16), ((t, ff), BF16), ((t, ff), BF16),
            ((rows, span, d), F32), ((rows, 8, d), F32),
        ] + gates_outs(rows, span, d, h),
        (x, xh, *sums, th, pa, u, cand, gain, taps, bias, masks, w_in, w_out, w_up, w_down),
        scratch=[pltpu.VMEM((span + 8, d), F32), pltpu.VMEM((t + 8 * rows, h), BF16)],
        name="middle",
    )


def mlp_back_part(
    l, span, gf, gl, gp, mid, u, c1, c2, gain, masks, w_out, w_up, w_down, pre_o, gmid_o, branch_o, reach_o, adj_o, sum_o, gain_o
):
    hidden = u.shape[1]
    ff = pre_o.shape[1]
    rows = gf.shape[0] // span
    gs = jnp.zeros(gf.shape, F32)
    for c in range(ff // STEP):
        lo, hi = c * STEP, (c + 1) * STEP
        pre = (dot(gl, w_down[l, lo:hi, :], 1, 1) * gp[:, lo:hi].astype(F32)).astype(BF16)
        pre_o[:, lo:hi] = pre
        gs = gs + dot(pre, w_up[l, :, lo:hi], 1, 1)
    m = mid[...]
    rr = rms(m)
    xhat = m * rr
    gain_o[...] = jnp.broadcast_to(jnp.sum(gs * xhat, axis=0, keepdims=True), gain_o.shape)
    e = gs * gain[l, 1:2, :]
    gm = gf + rr * (e - xhat * jnp.mean(e * xhat, axis=-1, keepdims=True))
    gmid_o[...] = gm
    branch = gm.astype(BF16)
    branch_o[...] = branch
    for c in range(hidden // CHUNK):
        lo, hi = c * CHUNK, (c + 1) * CHUNK
        gstate = dot(branch, w_out[l, lo:hi, :], 1, 1)
        for r in range(rows):
            base = r * span
            gst = gstate[base : base + span]

            def put(row, re, va, base=base, lo=lo, hi=hi, gst=gst):
                reach_o[base + row : base + row + 8, lo:hi] = re
                adj_o[base + row : base + row + 8, lo:hi] = gst[row : row + 8] + va

            re, va = scan_backward((1.0 - u[base : base + span, lo:hi]) * masks[r, 0:span, 1:2], gst, put)
            three = slice(base, base + 3)
            ad, rc = adj_o[three, lo:hi], reach_o[three, lo:hi]
            f1, f2 = c1[base : base + 8, lo:hi].astype(F32)[0:3], c2[base : base + 8, lo:hi].astype(F32)[0:3]
            re_hi, va_hi = low(re), low(va)
            sum_o[16 * r : 16 * r + 16, lo:hi] = jnp.concatenate(
                [ad * f1, rc * f1, ad * f2, rc * f2, re_hi, re - re_hi, va_hi, va - va_hi], axis=0
            ).astype(BF16)


def turn_body(l, blocks, x, *refs):
    sums = refs[:blocks]
    (
        th, pa, u, cand, c2, g, gain, masks, wo, wu, wd,
        state_o, c1_o, sec_o, act_o, mixed_o, pre_o, gmid_o, branch_o, reach_o, adj_o, sum_o, gain_o, mid, gp,
    ) = refs[blocks:]
    span = x.shape[1]
    out = mix_part(l, x, None, sums, th, pa, u, cand, gain, masks, wo, wu, wd, state_o, c1_o, mid, sec_o, act_o, gp)
    mixed_o[...] = out.astype(BF16).reshape(mixed_o.shape)
    gl = g[...]
    mlp_back_part(
        l, span, gl.astype(F32), gl, gp, mid, u, c1_o, c2, gain, masks, wo, wu, wd,
        pre_o, gmid_o, branch_o, reach_o, adj_o, sum_o, gain_o,
    )


def turn(l, x, sums, th, pa, u, cand, c2, g, gain, masks, w_out, w_up, w_down):
    rows, span, d = x.shape
    t, h = th.shape
    ff = w_up.shape[2]
    return call(
        functools.partial(turn_body, l, len(sums)),
        [((t, h), BF16), ((t, h), BF16), ((t, d), BF16), ((t, ff), BF16), ((rows, span, d), BF16)] + mlp_back_outs(rows, t, d, h, ff),
        (x, *sums, th, pa, u, cand, c2, g, gain, masks, w_out, w_up, w_down),
        scratch=[pltpu.VMEM((t, d), F32), pltpu.VMEM((t, ff), F32)],
        name="turn",
    )


def mlp_back_outs(rows, t, d, h, ff):
    return [
        ((t, ff), BF16), ((t, d), F32), ((t, d), BF16), ((t, h), F32), ((t, h), F32), ((16 * rows, h), BF16), ((8, d), F32),
    ]


def gates_back_part(
    l, x, xh, sums, reach, adj, c1, c2, gmid, gain_two, gain, taps, masks, w_in, proj, proj_o, tiny_o, ext, gext, small
):
    rows, span, d = x.shape
    t = rows * span
    hidden = c1.shape[1]
    kw = taps.shape[1]
    last = lax.axis_index("blk") == len(sums) - 1
    inside = jnp.logical_and(lax.broadcasted_iota(jnp.int32, (8, CHUNK), 0) < 3, jnp.logical_not(last))
    small[...] = jnp.zeros(small.shape, F32)
    small[1:2, :] = gain_two[0:1, :]
    for c in range(hidden // CHUNK):
        lo, hi = c * CHUNK, (c + 1) * CHUNK
        total = jnp.zeros((1, CHUNK), F32)
        halo = ([], [])
        for r in range(rows):
            base = r * span
            enter, after, edge = entering_backward(sums, r, lo, hi)
            ad = adj[base : base + span, lo:hi] + reach[base : base + span, lo:hi] * enter
            gl = ad * c1[base : base + span, lo:hi].astype(F32)
            total = total + jnp.sum(gl, axis=0, keepdims=True)
            proj[base : base + span, lo:hi] = gl.astype(BF16)
            proj[base : base + span, hidden + lo : hidden + hi] = (ad * c2[base : base + span, lo:hi].astype(F32)).astype(BF16)
            e0, e1 = edge[0:8], edge[8:16]
            lane1 = e0 + pltpu.roll(e0, 5, 0) * after
            second = jnp.concatenate([e0[6:8], e1[0:6]], axis=0)
            lane2 = second + pltpu.roll(second, 5, 0) * after
            halo[0].append(jnp.where(inside, lane1, 0.0))
            halo[1].append(jnp.where(inside, lane2, 0.0))
        for part in range(2):
            proj[t : t + 8 * rows, part * hidden + lo : part * hidden + hi] = jnp.concatenate(halo[part], axis=0).astype(BF16)
        at = 2 + kw + lo // d
        small[at : at + 1, lo % d : lo % d + CHUNK] = total
    proj_o[...] = proj[0:t, :]
    gci = dot(proj[...], w_in[l], 1, 1)
    g0 = gain[l, 0:1, :]
    out = []
    for r in range(rows):
        base = r * span
        xm = x[r].astype(F32)
        rr = rms(xm)
        xhat = xm * rr
        ext[8 : 8 + span, :] = low(xhat * g0)
        xv = xh[r].astype(F32)
        ext[0:8, :] = low(xv * rms(xv) * g0)
        gr = gci[base : base + span]
        gext[0:span, :] = gr
        gext[span : span + 8, :] = gci[t + 8 * r : t + 8 * r + 8]
        gn = gr * taps[l, 0:1, :]
        small[2:3, :] += jnp.sum(gr * ext[8 : 8 + span, :], axis=0, keepdims=True)
        for k in range(1, kw):
            gk = gr * masks[r, 0:span, k : k + 1]
            small[2 + k : 3 + k, :] += jnp.sum(gk * ext[8 - k : 8 - k + span, :], axis=0, keepdims=True)
            gn = gn + gext[k : k + span, :] * masks[r, k : k + span, k : k + 1] * taps[l, k : k + 1, :]
        small[0:1, :] += jnp.sum(gn * xhat, axis=0, keepdims=True)
        e = gn * g0
        out.append(gmid[base : base + span, :] + rr * (e - xhat * jnp.mean(e * xhat, axis=-1, keepdims=True)))
    for q in range(d // TINY):
        tiny_o[8 * q : 8 * q + 8, :] = small[:, q * TINY : (q + 1) * TINY]
    return jnp.concatenate(out, axis=0)


def back_scratch(rows, span, d, h):
    return [
        pltpu.VMEM((rows * (span + 8), 2 * h), BF16),
        pltpu.VMEM((span + 8, d), F32),
        pltpu.VMEM((span + 8, d), F32),
        pltpu.VMEM((8, d), F32),
    ]


def between_body(l, blocks, x, xh, *refs):
    sums = refs[:blocks]
    (
        reach, adj, c1, c2, gmid, gain_two, gp, mid, u, c1_next, c2_next, gain, taps, masks, wi, wo, wu, wd,
        proj_o, tiny_o, low_o, pre_o, gmid_o, branch_o, reach_o, adj_o, sum_o, gain_o, proj, ext, gext, small,
    ) = refs[blocks:]
    g = gates_back_part(
        l + 1, x, xh, sums, reach, adj, c1, c2, gmid, gain_two, gain, taps, masks, wi, proj, proj_o, tiny_o, ext, gext, small
    )
    gl = g.astype(BF16)
    low_o[...] = gl
    mlp_back_part(
        l, x.shape[1], g, gl, gp, mid, u, c1_next, c2_next, gain, masks, wo, wu, wd,
        pre_o, gmid_o, branch_o, reach_o, adj_o, sum_o, gain_o,
    )


def between(l, x, xh, sums, reach, adj, c1, c2, gmid, gain_two, gp, mid, u, c1_next, c2_next, gain, taps, masks, wi, wo, wu, wd, waits):
    rows, span, d = x.shape
    t, h, ff = rows * span, u.shape[1], gp.shape[1]
    return call(
        functools.partial(between_body, l, len(sums)),
        [((t, 2 * h), BF16), ((8 * d // TINY, TINY), F32), ((t, d), BF16)] + mlp_back_outs(rows, t, d, h, ff),
        (x, xh, *sums, reach, adj, c1, c2, gmid, gain_two, gp, mid, u, c1_next, c2_next, gain, taps, masks, wi, wo, wu, wd),
        scratch=back_scratch(rows, span, d, h),
        name="between",
        waits=waits,
    )


def final_body(l, blocks, x, xh, *refs):
    sums = refs[:blocks]
    reach, adj, c1, c2, gmid, gain_two, gain, taps, masks, wi, proj_o, tiny_o, gx_o, proj, ext, gext, small = refs[blocks:]
    g = gates_back_part(
        l, x, xh, sums, reach, adj, c1, c2, gmid, gain_two, gain, taps, masks, wi, proj, proj_o, tiny_o, ext, gext, small
    )
    gx_o[...] = g.astype(gx_o.dtype).reshape(gx_o.shape)


def final(l, x, xh, sums, reach, adj, c1, c2, gmid, gain_two, gain, taps, masks, wi, waits):
    rows, span, d = x.shape
    t, h = c1.shape
    return call(
        functools.partial(final_body, l, len(sums)),
        [((t, 2 * h), BF16), ((8 * d // TINY, TINY), F32), (x.shape, BF16)],
        (x, xh, *sums, reach, adj, c1, c2, gmid, gain_two, gain, taps, masks, wi),
        scratch=back_scratch(rows, span, d, h),
        name="final",
        waits=waits,
    )


def blocks_of(pairs, d):
    return [
        (i, a, b) for i, (left, right) in enumerate(pairs) for a in range(0, left.shape[1], d) for b in range(0, right.shape[1], d)
    ]


def part_body(blocks, d, tiny_rows, *refs):
    out = refs[-1]
    rows = out.shape[0]
    other = 1 - bit(0)
    for n, (i, a, b) in enumerate(blocks):
        at = pl.multiple_of(a + other * rows, rows)
        out[:, n * d : (n + 1) * d] = dot(refs[2 * i][:, pl.ds(at, rows)], refs[2 * i + 1][:, b : b + d], 0, 0).astype(BF16)
    if tiny_rows:
        lo = len(blocks) * d
        out[:, lo:] = jnp.zeros((rows, TINY), BF16)
        out[0:tiny_rows, lo:] = (refs[-2][...] * (other == 0).astype(F32)).astype(BF16)


def sum_body(blocks, d, tiny_rows, part, first, *refs):
    other, keep_o, send_o = refs[-3:]
    rows = other.shape[0]
    half = rows // 2
    cut = len(blocks) // 2
    core = bit(0)
    mine = bit(first)
    for out, take in ((send_o, 1 - mine), (keep_o, mine)):
        here = rows_at(take, half)
        for n in range(part * cut, (part + 1) * cut):
            i, a, b = blocks[n]
            at = pl.multiple_of(a + core * rows + take * half, half)
            got = other[here, n * d : (n + 1) * d].astype(F32)
            col = (n - part * cut) * d
            out[:, col : col + d] = (dot(refs[2 * i][:, pl.ds(at, half)], refs[2 * i + 1][:, b : b + d], 0, 0) + got).astype(BF16)
        if tiny_rows and part == 1:
            lo, col = len(blocks) * d, cut * d
            out[:, col:] = other[here, lo:]
            here0 = jnp.logical_and(core == 0, take == 0).astype(F32)
            out[0:tiny_rows, col:] = (
                other[pl.ds(pl.multiple_of(take * half, half), tiny_rows), lo:].astype(F32) + refs[-4][...] * here0
            ).astype(BF16)


def whole_body(blocks, d, *refs):
    out = refs[-1]
    for n, (i, a, b) in enumerate(blocks):
        out[:, n * d : (n + 1) * d] = dot(refs[2 * i][:, a : a + d], refs[2 * i + 1][:, b : b + d], 0, 0).astype(BF16)


def whole(pairs, d):
    blocks = blocks_of(pairs, d)
    flat = [m for pair in pairs for m in pair]
    return call(functools.partial(whole_body, blocks, d), [((d, len(blocks) * d), BF16)], flat, name="whole", limit=12)[0]


def part(pairs, tiny, d, waits):
    blocks = blocks_of(pairs, d)
    flat = [m for pair in pairs for m in pair] + ([tiny] if tiny is not None else [])
    wide = len(blocks) * d + (0 if tiny is None else TINY)
    body = functools.partial(part_body, blocks, d, 0 if tiny is None else tiny.shape[0])
    return call(body, [((d // 2, wide), BF16)], flat, name="part", waits=waits)[0]


def part_sums(pairs, tiny, got, which, first, d, waits):
    blocks = blocks_of(pairs, d)
    flat = [m for pair in pairs for m in pair] + ([tiny] if tiny is not None else [])
    extra = 0 if tiny is None or which == 0 else TINY
    shape = (d // 4, len(blocks) * d // 2 + extra)
    body = functools.partial(sum_body, blocks, d, 0 if tiny is None else tiny.shape[0], which, first)
    return call(body, [(shape, BF16)] * 2, (*flat, got), name="sum", waits=waits)


def add_rows(keep, got, where):
    return (keep[where, :].astype(F32) + got[where, :].astype(F32)).astype(BF16)


def add_body(k, keep, got, keep_o, send_o):
    half = keep_o.shape[0]
    mine = bit(k)
    send_o[...] = add_rows(keep, got, rows_at(1 - mine, half))
    keep_o[...] = add_rows(keep, got, rows_at(mine, half))


def add_split(keep, got, k, waits=()):
    shape = (keep.shape[0] // 2, keep.shape[1])
    return call(functools.partial(add_body, k), [(shape, BF16)] * 2, (keep, got), name="add", limit=4, waits=waits)


def add_both_body(k, keep_a, got_a, keep_b, got_b, keep_o, send_o):
    half = keep_o.shape[0]
    cut = keep_a.shape[1]
    mine = bit(k)
    for out, which in ((send_o, 1 - mine), (keep_o, mine)):
        out[:, :cut] = add_rows(keep_a, got_a, rows_at(which, half))
        out[:, cut:] = add_rows(keep_b, got_b, rows_at(which, half))


def add_both(keep_a, got_a, keep_b, got_b, k, waits=()):
    shape = (keep_a.shape[0] // 2, keep_a.shape[1] + keep_b.shape[1])
    return call(
        functools.partial(add_both_body, k), [(shape, BF16)] * 2, (keep_a, got_a, keep_b, got_b), name="add_both", limit=4, waits=waits
    )


def add_whole_body(keep, got, out):
    out[...] = add_rows(keep, got, slice(None))


def add_whole(keep, got, waits=()):
    return call(add_whole_body, [(keep.shape, BF16)], (keep, got), name="add_whole", limit=4, waits=waits)[0]


def join_body(k, own, other, *outs):
    rows = own.shape[0]
    mine = bit(k)
    lo = 0
    for out in outs:
        hi = lo + out.shape[1]
        out[rows_at(mine, rows), :] = own[:, lo:hi]
        out[rows_at(1 - mine, rows), :] = other[:, lo:hi]
        lo = hi


def join(own, other, k, cut=None, waits=()):
    rows, cols = own.shape
    widths = [cols] if cut is None else [cut, cols - cut]
    return call(functools.partial(join_body, k), [((2 * rows, w), BF16) for w in widths], (own, other), name="join", limit=4, waits=waits)


BITS = ((2, 1), (1, 2))
REST = (3, 4)
GROUPS = {'a': (((1, 'down'),), None), 'b': (((1, 'up'), (1, 'out')), None), 'c': (((1, 'in'), (0, 'down'), (0, 'out')), 1), 'd': (((0, 'up'), (0, 'in')), 0)}
TIED = True
STEPS = [
    "b+", "a+", "bp0", "bp1", "ap0", "ap1", "between", "c+", "b10", "b11", "a11", "final", "a10", "bz0", "d+", "cp1",
    "bz1", "dp1", "az0", "cp0", "az1", "bt", "c11", "dp0", "at", "c10", "bj", "bJ", "aj", "cz0", "cz1", "d10", "aJ",
    "d11", "ct", "b21", "a21", "a20", "b20", "cj", "af0", "dz0", "cJ", "af1", "dz1", "bf0", "c21", "c20", "dt", "dj",
    "bf1", "dJ", "aS", "d21", "cf0", "d20", "cf1", "cS", "df1", "df0", "dS", "bS",
]


class Group:
    def __init__(self, pairs, tiny, d, n, waits):
        self.pairs, self.tiny, self.d, self.n = pairs, tiny, d, n
        self.sent = part(pairs, tiny, d, waits)
        self.other = self.flip(self.sent, 0)
        self.cut = len(blocks_of(pairs, d)) // 2 * d
        self.keep, self.got, self.mine, self.theirs = ([None, None] for _ in range(4))

    def flip(self, value, k):
        return lax.ppermute(value, AXES, [(i, i ^ (1 << k)) for i in range(self.n)])

    def step(self, op, waits):
        keep, got = self.keep, self.got
        if op[0] == "p":
            p = int(op[1])
            keep[p], send = part_sums(self.pairs, self.tiny, self.other, p, BITS[p][0], self.d, waits)
            got[p] = self.flip(send, BITS[p][0])
            return send
        if op[0] == "1":
            p = int(op[1])
            keep[p], send = add_split(keep[p], got[p], BITS[p][1], waits)
            got[p] = self.flip(send, BITS[p][1])
            return send
        if op == "z0":
            self.row, send = add_both(keep[0], got[0], keep[1], got[1], REST[0], waits)
            self.far = self.flip(send, REST[0])
            return send
        if op == "z1":
            self.row, send = add_split(self.row, self.far, REST[1], waits)
            self.far = self.flip(send, REST[1])
            return send
        if op == "t":
            total = add_whole(self.row, self.far, waits)
            for k in range(5, self.n.bit_length() - 1):
                total = add_whole(total, self.flip(total, k))
            self.row = total
            self.far = self.flip(total, REST[1])
            return total
        if op == "j":
            (self.row,) = join(self.row, self.far, REST[1], None, waits)
            self.far = self.flip(self.row, REST[0])
            return self.row
        if op == "J":
            self.keep = list(join(self.row, self.far, REST[0], self.cut, waits))
            self.got = [self.flip(self.keep[p], BITS[p][1]) for p in range(2)]
            return self.keep[1]
        p = int(op[1])
        if op[0] == "2":
            (keep[p],) = join(keep[p], got[p], BITS[p][1], None, waits)
            got[p] = self.flip(keep[p], BITS[p][0])
            return keep[p]
        (self.mine[p],) = join(keep[p], got[p], BITS[p][0], None, waits)
        self.theirs[p] = self.flip(self.mine[p], 0)
        return self.mine[p]


SLOTS = 6


def spread_body(places, d, tiny_rows, count, aliased, cut, *refs):
    pieces = refs[:4]
    at = len(pieces) + aliased
    tiny_in = refs[at] if tiny_rows == 2 else None
    at += 1 if tiny_rows == 2 else 0
    outs = refs[at : at + count]
    tiny_outs = refs[at + count : -4]
    token_o, stage, tiny_all, sem = refs[-4:]
    token_o[...] = jnp.zeros(token_o.shape, F32)
    rows = stage.shape[1]
    flying = [None] * SLOTS
    todo = []
    for n, place in enumerate(places):
        part = n // cut
        for k in range(2):
            todo.append((pieces[2 * part + k], (n - part * cut) * d, (bit(0) if k == 0 else 1 - bit(0)) * rows, place))
    for step, (piece, col, row, (out, l, r, c)) in enumerate(todo):
        slot = step % SLOTS
        if flying[slot] is not None:
            flying[slot].wait()
        stage[slot] = piece[:, col : col + d].astype(F32)
        there = outs[out].at[l, pl.ds(pl.multiple_of(r + row, rows), rows), pl.ds(c, d)]
        flying[slot] = fetch(stage.at[slot], there, sem.at[slot])
    if tiny_rows:
        lo = cut * d
        for k in range(2):
            core = bit(0) if k == 0 else 1 - bit(0)
            tiny_all[pl.ds(pl.multiple_of(core * rows, rows), rows), :] = pieces[2 + k][:, lo:].astype(F32)
    if tiny_rows == 1:
        for q in range(d // TINY):
            tiny_outs[0][:, q * TINY : (q + 1) * TINY] = tiny_all[8 * q : 8 * q + 8, :]
    if tiny_rows == 2:
        gain_o, taps_o, bias_o = tiny_outs
        kw = taps_o.shape[1]
        for q in range(d // TINY):
            lo, hi = q * TINY, (q + 1) * TINY
            for layer in range(2):
                own = tiny_all[8 * q : 8 * q + 8, :] if layer == 0 else tiny_in[:, lo:hi]
                gain_o[layer, :, lo:hi] = own[0:2]
                taps_o[layer, :, lo:hi] = own[2 : 2 + kw]
                for b in range(bias_o.shape[1] // d):
                    bias_o[layer : layer + 1, b * d + lo : b * d + hi] = own[2 + kw + b : 3 + kw + b]
    for copy in flying:
        if copy is not None:
            copy.wait()


def spread(pieces, places, shapes, old, tiny_in, tiny_kind, tiny_shapes, d, waits):
    args = [*pieces]
    aliases = {}
    for i, o in enumerate(old):
        if o is not None:
            aliases[len(args)] = i
            args.append((HBM, o))
    if tiny_kind == 2:
        args.append(tiny_in)
    rows = d // 2
    cut = len(places) // 2
    return call(
        functools.partial(spread_body, places, d, tiny_kind, len(shapes), len(aliases), cut),
        [(HBM, s, F32) for s in shapes] + [(s, F32) for s in tiny_shapes] + [((8, TINY), F32)],
        args,
        scratch=[
            pltpu.VMEM((SLOTS, rows, d), F32),
            pltpu.VMEM((2 * rows, TINY), F32),
            pltpu.SemaphoreType.DMA((SLOTS,)),
        ],
        aliases=aliases,
        name="spread",
        waits=waits,
    )


def passed_along(block, axis, distance):
    devices = range(lax.axis_size(axis))
    route = [(i - distance, i) for i in devices if i - distance in devices]
    return lax.ppermute(block, axis, route)


def from_blocks(value):
    size = lax.axis_size("blk")
    got = {0: value}
    far = size >> 1
    while far:
        for k, v in list(got.items()):
            got[k | far] = lax.ppermute(v, "blk", [(i, i ^ far) for i in range(size)])
        far >>= 1
    return [got[k] for k in range(size)]


def shards(
    hidden_in, cotangent, lengths, norm_gain, conv_weight, gate_bias, in_weight, out_weight, up_weight, down_weight
):
    rows, span, d = hidden_in.shape
    h = gate_bias.shape[1]
    ff = up_weight.shape[2]
    blocks = lax.axis_size("blk")
    n = lax.axis_size("batch") * blocks
    groups = {}
    made = {}

    xh0 = passed_along(hidden_in[:, span - 8 :], "blk", 1)
    x0, gain, taps, bias, wi, masks = load(hidden_in, lengths, norm_gain, conv_weight, gate_bias, in_weight)
    u0, cand, c20, th, pa, conv0, sums, wo, wu, wd = gates(
        0, x0, xh0, gain, taps, bias, masks, wi, (out_weight, up_weight, down_weight)
    )
    state0, c10, mid0, sec0, act0, gp0, x1, xh1, u1, cand, c21, th, pa, conv1, sums = middle(
        0, x0, xh0, from_blocks(sums), th, pa, u0, cand, gain, taps, bias, masks, wi, wo, wu, wd
    )
    g = cotangent.reshape(rows * span, d)
    state1, c11, sec1, act1, mixed, pre1, gmid1, branch1, reach, adj, sums, gain_two = turn(
        1, x1, from_blocks(sums), th, pa, u1, cand, c21, g, gain, masks, wo, wu, wd
    )
    made[1, "down"], made[1, "up"], made[1, "out"] = (act1, g), (sec1, pre1), (state1, branch1)

    counts = {"down": ff // d, "up": ff // d, "out": h // d, "in": 2 * h // d}
    shapes = {"down": down_weight.shape, "up": up_weight.shape, "out": out_weight.shape, "in": in_weight.shape}
    small_shapes = [norm_gain.shape, conv_weight.shape, gate_bias.shape]
    out = {}

    def write(name, waits):
        kinds, tiny = GROUPS[name]
        group = groups[name]
        pieces = [group.mine[0], group.theirs[0], group.mine[1], group.theirs[1]]
        places = [
            (k, layer, j * d, 0) if kind in ("down", "out") else (k, layer, 0, j * d)
            for k, (layer, kind) in enumerate(kinds)
            for j in range(counts[kind])
        ]
        old = [out.get(kind) for _, kind in kinds]
        tiny_kind = 0 if tiny is None else 1 if "small" not in out else 2
        got = spread(
            pieces, places, [shapes[kind] for _, kind in kinds], old, out.get("small"), tiny_kind,
            [[], [(8, d)], small_shapes][tiny_kind], d, waits,
        )
        for (_, kind), value in zip(kinds, got):
            out[kind] = value
        if tiny_kind == 1:
            out["small"] = got[-2]
        if tiny_kind == 2:
            out["gain"], out["conv"], out["bias"] = got[-4:-1]
        return got[-1]

    latest = []
    for op in STEPS:
        waits = latest if TIED else []
        if op == "between":
            proj1, tiny1, low0, pre0, gmid0, branch0, reach, adj, sums, gain_two = between(
                0, x1, xh1, from_blocks(sums), reach, adj, c11, c21, gmid1, gain_two, gp0, mid0, u0, c10, c20,
                gain, taps, masks, wi, wo, wu, wd, waits,
            )
            made[1, "in"], made[1, "tiny"] = (conv1, proj1), tiny1
            made[0, "down"], made[0, "up"], made[0, "out"] = (act0, low0), (sec0, pre0), (state0, branch0)
            latest = [tiny1]
        elif op == "final":
            proj0, tiny0, input_grad = final(
                0, x0, xh0, from_blocks(sums), reach, adj, c10, c20, gmid0, gain_two, gain, taps, masks, wi, waits
            )
            made[0, "in"], made[0, "tiny"] = (conv0, proj0), tiny0
            latest = [tiny0]
        elif op[1] == "+":
            kinds, tiny = GROUPS[op[0]]
            groups[op[0]] = Group([made[key] for key in kinds], None if tiny is None else made[tiny, "tiny"], d, n, waits)
            latest = [groups[op[0]].sent]
        elif op[1] == "S":
            latest = [write(op[0], waits)]
        else:
            latest = [groups[op[0]].step(op[1:], waits)]
    return (mixed, input_grad, out["gain"], out["conv"], out["bias"], out["in"], out["out"], out["up"], out["down"])


def solution(mesh):
    row = P("batch", "blk", None)
    return jax.shard_map(
        shards,
        mesh=mesh,
        in_specs=(row, row, P("batch", None)) + (P(),) * 7,
        out_specs=(row, row) + (P(),) * 7,
        check_vma=False,
    )
```
